256 devices in a mesh: row: 4 (over z_hi), col: 64 (over x, z_lo, y, core).
Axes of the slice: x: 4, y: 4, z: 8 (z_hi: 4, z_lo: 2; z = z_hi * 2 + z_lo), core: 2. Of those that a mesh axis runs over, the one named last changes fastest.
Arguments:
- gradient: bfloat16 [2048, 8192], P('row', 'col'), may hold values from -6 to 6
- first_moment: float32 [2048, 8192], P('row', 'col'), may hold values from -2 to 2
- second_moment: float32 [2048, 8192], P('row', 'col'), may hold values from 0.05 to 2
- left_basis: bfloat16 [2048, 2048], P('col', 'row'), may hold values from -0.125 to 0.125
- right_basis: bfloat16 [8192, 8192], P('row', 'col'), may hold values from -0.0625 to 0.0625
Outputs:
- update: float32 [2048, 8192], P('row', 'col')
- first_new: float32 [2048, 8192], P('row', 'col')
- second_new: float32 [2048, 8192], P('row', 'col')
The draws below stay inside these ranges and needn't reach their ends.
All inputs are finite; a program needn't handle non-finite values.
Results may differ from the reference program's by a relative error of at most 0.004.
Values may be sent and summed in bfloat16 or wider, within the bound.
A program may use at most 64 MiB of HBM per device.

```python
import math
import jax
import jax.numpy as jnp

M = 2048
N = 8192
STEP = 10


def levels(rng, dims, shards, low, high):
    gain, own = 1.0, jax.random.fold_in(rng, 6)
    for position, blocks in shards:
        steps = jnp.exp(jax.random.uniform(jax.random.fold_in(own, position), (blocks,), jnp.float32, low / len(shards), high / len(shards)))
        gain = gain * jnp.repeat(steps, dims[position] // blocks).reshape([-1 if axis == position else 1 for axis in range(len(dims))])
    return gain


def scatter_about(own_key, extent, spread, limit, cuts=(), held_as=jnp.bfloat16):
    entries = jax.random.normal(own_key, extent, jnp.float32) * spread
    if len(cuts) > 0:
        entries = levels(own_key, extent, cuts, -0.22, 0.18) * entries
    return jnp.clip(entries, min=-limit, max=limit).astype(held_as)


def setup_inputs(seed: int = 0) -> dict:
    key_of = jax.random.split(jax.random.key(seed), 6)
    return {
        "gradient": scatter_about(key_of[0], (M, N), 1.0, 6.0, ((0, 4), (1, 64))),
        "first_moment": scatter_about(key_of[1], (M, N), 0.3, 2.0, ((0, 4), (1, 64)), jnp.float32),
        "second_moment": jnp.clip(jnp.exp(math.log(2.0) - 3.6888794 * jax.random.uniform(key_of[2], (M, N), jnp.float32) ** levels(key_of[2], (M, N), ((0, 4), (1, 64)), -0.2, 0.2)), 0.05, 2.0),
        "left_basis": scatter_about(key_of[3], (M, M), M ** -0.5, 0.125, ((0, 64), (1, 4))),
        "right_basis": scatter_about(key_of[4], (N, N), N ** -0.5, 0.0625, ((0, 4), (1, 64))),
    }


beta_one = 0.9
beta_two = 0.95
epsilon = 1e-08

def reference(gradient, first_moment, second_moment, left_basis, right_basis):
    turned = jnp.dot(gradient, right_basis, preferred_element_type=jnp.float32).astype(jnp.bfloat16)
    rotated = jnp.dot(left_basis.T, turned, preferred_element_type=jnp.float32)
    first_new = beta_one * first_moment + (1.0 - beta_one) * rotated
    second_new = beta_two * second_moment + (1.0 - beta_two) * rotated * rotated
    corrected_one = first_new / (1.0 - beta_one ** STEP)
    corrected_two = second_new / (1.0 - beta_two ** STEP)
    scaled = (corrected_one / (jnp.sqrt(corrected_two) + epsilon)).astype(jnp.bfloat16)
    back_half = jnp.dot(left_basis, scaled, preferred_element_type=jnp.float32).astype(jnp.bfloat16)
    update = jnp.dot(back_half, right_basis.T, preferred_element_type=jnp.float32)
    return (update, first_new, second_new)
```

```python
import functools

import jax
import jax.numpy as jnp
from jax import lax
from jax.experimental import pallas as pl
from jax.experimental.pallas import tpu as pltpu
from jax.sharding import PartitionSpec as P

STEP = 10
beta_one = 0.9
beta_two = 0.95
epsilon = 1e-08

MESH = pl.DeviceIdType.MESH
F32 = jnp.float32
BF16 = jnp.bfloat16
SLOTS = 112


def kernel(g, l, r, m, v, upd, fo, so, Gb, Lb, Rb, Rs, Tt, Qb, Bp, Bm, Sb, Ba, Bk, Bs,
           Vb, Rd, W, X, Fb, mb, vb, fb, sb, ssem, rsem, lsem):
    zh = lax.axis_index("row")
    col = lax.axis_index("col")
    c = col % 2
    y = (col // 2) % 4
    zl = (col // 8) % 2
    x = col // 16
    z = 2 * zh + zl

    def dev(x_, y_, z_, c_):
        return (z_ // 2, ((x_ * 2 + z_ % 2) * 4 + y_) * 2 + c_)

    def xn(d):
        return dev((x + d) % 4, y, z, c)

    def yn(d):
        return dev(x, (y + d) % 4, z, c)

    def zn(d):
        return dev(x, y, (z + d) % 8, c)

    sib = dev(x, y, z, 1 - c)
    pair = dev(x, y, 2 * zh + 1 - zl, c)
    g_to = dev(2 * (zh % 2) + 1 - zl, y, 2 * x + zh // 2, c)
    g_from = dev(zh, y, 2 * (2 * zl + x // 2) + 1 - x % 2, c)
    l_xp = 2 * (x % 2) + 1 - zl
    l_to = [dev(l_xp, y, 2 * ((zh + d) % 4) + x // 2, c) for d in range(4)]
    l_from = [dev(2 * zl + x // 2, y, 2 * ((zh + 4 - d) % 4) + 1 - x % 2, c) for d in range(4)]

    slots = {}
    sent = []

    def slot(name):
        return slots.setdefault(name, len(slots))

    def send(name, src, dst, to):
        k = slot(name)
        copy = pltpu.make_async_remote_copy(
            src_ref=src, dst_ref=dst, send_sem=ssem.at[k], recv_sem=rsem.at[k],
            device_id=to, device_id_type=MESH)
        copy.start()
        sent.append(copy)

    def recv(name, dst):
        k = slot(name)
        pltpu.make_async_remote_copy(
            src_ref=dst, dst_ref=dst, send_sem=ssem.at[k], recv_sem=rsem.at[k],
            device_id=sib, device_id_type=MESH).wait_recv()

    own = [
        pltpu.make_async_copy(r, Rb.at[zl], lsem.at[0]),
        pltpu.make_async_copy(m, mb, lsem.at[1]),
        pltpu.make_async_copy(v, vb, lsem.at[2]),
    ]
    for copy in own:
        copy.start()

    barrier = pltpu.get_barrier_semaphore()
    partners = [g_to, g_from, sib, zn(1), zn(7)] + l_to + l_from
    partners += [xn(d) for d in (1, 2, 3)] + [yn(d) for d in (1, 2, 3)]
    for p in partners:
        pl.semaphore_signal(barrier, inc=1, device_id=p, device_id_type=MESH)
    pl.semaphore_wait(barrier, len(partners))

    g_xp = 2 * (zh % 2) + 1 - zl
    for h in range(2):
        send(("gp", h), g.at[h], Gb.at[g_xp, y, c, h], g_to)
    lcols = pl.ds(pl.multiple_of(zh * 512, 512), 512)
    for d in range(4):
        send(("lp", d), l, Lb.at[l_xp, y, c, :, lcols], l_to[d])
    send("rs0", r.at[:, 1 - c], Rs.at[zl], sib)

    recv(("gp", 0), Gb.at[x, y, c, 0])
    for d in (2, 1, 3):
        send(("gx", d), Gb.at[x, y, c, 0], Gb.at[x, y, c, 0], xn(d))
    recv(("gp", 1), Gb.at[x, y, c, 1])
    for d in (2, 1, 3):
        send(("gy", d), Gb.at[x, y, c, 1], Gb.at[x, y, c, 1], yn(d))
    send("rp", r, Rb.at[zl], pair)
    for d in range(4):
        src_zh = (zh + 4 - d) % 4
        recv(("lp", d), Lb.at[x, y, c, :, pl.ds(pl.multiple_of(src_zh * 512, 512), 512)])

    lh = [pl.ds(0, 1024), pl.ds(1024, 1024)]

    for d in (1, 3, 2):
        recv(("gx", d), Gb.at[(x + 4 - d) % 4, y, c, 0])
    lo, hi = pl.ds(0, 2), pl.ds(2, 2)
    send("Gy1a", Gb.at[lo, y, c, 0], Gb.at[lo, y, c, 0], yn(1))
    send("Gy3b", Gb.at[hi, y, c, 0], Gb.at[hi, y, c, 0], yn(3))
    send("Gy1b", Gb.at[hi, y, c, 0], Gb.at[hi, y, c, 0], yn(1))
    send("Gy3a", Gb.at[lo, y, c, 0], Gb.at[lo, y, c, 0], yn(3))
    send("Gs0", Gb.at[:, y, c, 0], Gb.at[:, y, c, 0], sib)
    for d in (1, 3, 2):
        recv(("gy", d), Gb.at[x, (y + 4 - d) % 4, c, 1])
    send("Gx1a", Gb.at[x, lo, c, 1], Gb.at[x, lo, c, 1], xn(1))
    send("Gx3b", Gb.at[x, hi, c, 1], Gb.at[x, hi, c, 1], xn(3))
    send("Gx1b", Gb.at[x, hi, c, 1], Gb.at[x, hi, c, 1], xn(1))
    send("Gx3a", Gb.at[x, lo, c, 1], Gb.at[x, lo, c, 1], xn(3))
    send("Gs1", Gb.at[x, :, c, 1], Gb.at[x, :, c, 1], sib)
    for d in (2, 1, 3):
        send(("lx", d), Lb.at[x, y, c, :, lh[0]], Lb.at[x, y, c, :, lh[0]], xn(d))
        send(("ly", d), Lb.at[x, y, c, :, lh[1]], Lb.at[x, y, c, :, lh[1]], yn(d))

    xm, xp, x2 = (x + 3) % 4, (x + 1) % 4, (x + 2) % 4
    ym, yp, y2 = (y + 3) % 4, (y + 1) % 4, (y + 2) % 4
    recv("Gy1a", Gb.at[lo, ym, c, 0])
    send("Gyfa", Gb.at[lo, ym, c, 0], Gb.at[lo, ym, c, 0], yn(1))
    recv("Gy3b", Gb.at[hi, yp, c, 0])
    send("Gyfb", Gb.at[hi, yp, c, 0], Gb.at[hi, yp, c, 0], yn(3))
    recv("Gx1a", Gb.at[xm, lo, c, 1])
    send("Gxfa", Gb.at[xm, lo, c, 1], Gb.at[xm, lo, c, 1], xn(1))
    recv("Gx3b", Gb.at[xp, hi, c, 1])
    send("Gxfb", Gb.at[xp, hi, c, 1], Gb.at[xp, hi, c, 1], xn(3))
    recv("Gy1b", Gb.at[hi, ym, c, 0])
    send("Gs2", Gb.at[:, ym, c, 0], Gb.at[:, ym, c, 0], sib)
    recv("Gy3a", Gb.at[lo, yp, c, 0])
    send("Gs3", Gb.at[:, yp, c, 0], Gb.at[:, yp, c, 0], sib)
    recv("Gx1b", Gb.at[xm, hi, c, 1])
    send("Gs4", Gb.at[xm, :, c, 1], Gb.at[xm, :, c, 1], sib)
    recv("Gx3a", Gb.at[xp, lo, c, 1])
    send("Gs5", Gb.at[xp, :, c, 1], Gb.at[xp, :, c, 1], sib)

    def lrow(i, h):
        return Lb.at[:, i, c, :, lh[h]]

    def lpart(a, b, h):
        return Lb.at[a, b, c, :, lh[h]]

    for d in (1, 3, 2):
        recv(("lx", d), lpart((x + 4 - d) % 4, y, 0))
    for d in (1, 3, 2):
        recv(("ly", d), lpart(x, (y + 4 - d) % 4, 1))
    for name, a, b, h, to in (
            ("Ly1a", lo, y, 0, yn(1)), ("Ly3b", hi, y, 0, yn(3)),
            ("Lx1a", x, lo, 1, xn(1)), ("Lx3b", x, hi, 1, xn(3)),
            ("Ly1b", hi, y, 0, yn(1)), ("Ly3a", lo, y, 0, yn(3)),
            ("Lx1b", x, hi, 1, xn(1)), ("Lx3a", x, lo, 1, xn(3))):
        send(name, lpart(a, b, h), lpart(a, b, h), to)
    send("Ls0", lpart(slice(None), y, 0), lpart(slice(None), y, 0), sib)
    send("Ls1", lpart(x, slice(None), 1), lpart(x, slice(None), 1), sib)

    recv("Gyfa", Gb.at[lo, y2, c, 0])
    recv("Gyfb", Gb.at[hi, y2, c, 0])
    send("Gs6", Gb.at[:, y2, c, 0], Gb.at[:, y2, c, 0], sib)
    recv("Gxfa", Gb.at[x2, lo, c, 1])
    recv("Gxfb", Gb.at[x2, hi, c, 1])
    send("Gs7", Gb.at[x2, :, c, 1], Gb.at[x2, :, c, 1], sib)
    recv("rp", Rb.at[1 - zl])
    send("rs1", Rb.at[1 - zl, :, 1 - c], Rs.at[1 - zl], sib)

    recv("Ly1a", lpart(lo, ym, 0))
    send("Lyfa", lpart(lo, ym, 0), lpart(lo, ym, 0), yn(1))
    recv("Ly3b", lpart(hi, yp, 0))
    send("Lyfb", lpart(hi, yp, 0), lpart(hi, yp, 0), yn(3))
    recv("Lx1a", lpart(xm, lo, 1))
    send("Lxfa", lpart(xm, lo, 1), lpart(xm, lo, 1), xn(1))
    recv("Lx3b", lpart(xp, hi, 1))
    send("Lxfb", lpart(xp, hi, 1), lpart(xp, hi, 1), xn(3))

    o = 1 - c
    recv("Gs0", Gb.at[:, y, o, 0])
    recv("Gs2", Gb.at[:, ym, o, 0])
    recv("Gs3", Gb.at[:, yp, o, 0])
    recv("Gs6", Gb.at[:, y2, o, 0])
    own[0].wait()

    def turn(b, h):
        lhs = jnp.concatenate(
            [Gb[2 * b + 1 - i, j, k, h] for i in range(2) for j in range(4) for k in range(2)], axis=1)
        rhs = jnp.concatenate([Rb[i].reshape(2048, 128) for i in range(2)], axis=1)
        t = jnp.dot(lhs, rhs, preferred_element_type=F32)
        q = 2 * b + 1 - h
        Tt[:, q * 256:(q + 1) * 256] = t.T.astype(BF16)

    turn(0, 0)
    turn(1, 0)
    recv("Gs1", Gb.at[x, :, o, 1])
    recv("Gs4", Gb.at[xm, :, o, 1])
    recv("Gs5", Gb.at[xp, :, o, 1])
    recv("Gs7", Gb.at[x2, :, o, 1])
    turn(0, 1)
    turn(1, 1)

    recv("Ly1b", lpart(hi, ym, 0))
    send("Ls2", lpart(slice(None), ym, 0), lpart(slice(None), ym, 0), sib)
    recv("Ly3a", lpart(lo, yp, 0))
    send("Ls3", lpart(slice(None), yp, 0), lpart(slice(None), yp, 0), sib)
    recv("Lx1b", lpart(xm, hi, 1))
    send("Ls4", lpart(xm, slice(None), 1), lpart(xm, slice(None), 1), sib)
    recv("Lx3a", lpart(xp, lo, 1))
    send("Ls5", lpart(xp, slice(None), 1), lpart(xp, slice(None), 1), sib)
    recv("Lyfa", lpart(lo, y2, 0))
    recv("Lyfb", lpart(hi, y2, 0))
    send("Ls6", lpart(slice(None), y2, 0), lpart(slice(None), y2, 0), sib)
    recv("Lxfa", lpart(x2, lo, 1))
    recv("Lxfb", lpart(x2, hi, 1))
    send("Ls7", lpart(x2, slice(None), 1), lpart(x2, slice(None), 1), sib)

    def other(a, b, h):
        return Lb.at[a, b, o, :, lh[h]]

    recv("Ls0", other(slice(None), y, 0))
    recv("Ls2", other(slice(None), ym, 0))
    recv("Ls3", other(slice(None), yp, 0))
    recv("Ls6", other(slice(None), y2, 0))
    recv("Ls1", other(x, slice(None), 1))
    recv("Ls4", other(xm, slice(None), 1))
    recv("Ls5", other(xp, slice(None), 1))
    recv("Ls7", other(x2, slice(None), 1))

    def left(k):
        cols = pl.ds(pl.multiple_of(k * 512, 512), 512)
        return Lb[:, :, :, :, cols].reshape(1024, 512)

    def rotate(d):
        k = (zh + d) % 4
        q = jnp.dot(Tt[...], left(k), preferred_element_type=F32)
        Qb[2 * k, 0] = q[0:64].astype(BF16)
        Qb[2 * k, 1] = q[64:128].astype(BF16)
        Qb[2 * k + 1, 0] = q[128:192].astype(BF16)
        Qb[2 * k + 1, 1] = q[192:256].astype(BF16)

    def zi(d):
        return (z + d) % 8

    rotate(2)
    send(("bp", 1, 0), Qb.at[zi(4), 0], Bp.at[0, 0], zn(1))
    send(("bm", 1, 1), Qb.at[zi(4), 1], Bm.at[0, 1], zn(7))
    rotate(1)
    rotate(3)
    send(("bp", 2, 1), Qb.at[zi(3), 1], Bp.at[1, 1], zn(1))
    send(("bm", 2, 0), Qb.at[zi(5), 0], Bm.at[1, 0], zn(7))
    rotate(0)

    def add(k, i, buf, s):
        Qb[k, i] = (Qb[k, i].astype(F32) + buf[s, i].astype(F32)).astype(BF16)

    for s, order in ((2, (0,)), (3, (1, 0)), (4, (1, 0))):
        for i in order:
            j = i
            recv(("bp", s - 1, j), Bp.at[s - 2, j])
            add(zi(5 - s), j, Bp, s - 2)
            send(("bp", s, j), Qb.at[zi(5 - s), j], Bp.at[s - 1, j], zn(1))
            j = 1 - i
            recv(("bm", s - 1, j), Bm.at[s - 2, j])
            add(zi(3 + s), j, Bm, s - 2)
            send(("bm", s, j), Qb.at[zi(3 + s), j], Bm.at[s - 1, j], zn(7))
    own[1].wait()
    own[2].wait()
    for i in range(2):
        recv(("bp", 4, i), Bp.at[3, i])
        recv(("bm", 4, i), Bm.at[3, i])
    total = Qb[z].reshape(128, 512).astype(F32) + Bp[3].reshape(128, 512).astype(F32) \
        + Bm[3].reshape(128, 512).astype(F32)
    rotated = total.T
    first = beta_one * mb[...] + (1.0 - beta_one) * rotated
    second = beta_two * vb[...] + (1.0 - beta_two) * rotated * rotated
    one = first * (1.0 / (1.0 - beta_one**STEP))
    two = second * (1.0 / (1.0 - beta_two**STEP))
    scaled = (one / (jnp.sqrt(two) + epsilon)).astype(BF16)
    Sb[z, 0] = scaled[0:256]
    Sb[z, 1] = scaled[256:512]
    for i in range(2):
        send(("cp", 1, i), Sb.at[z, i], Sb.at[z, i], zn(1))
        send(("cm", 1, i), Sb.at[z, i], Sb.at[z, i], zn(7))
    fb[...] = first
    sb[...] = second
    outs = [pltpu.make_async_copy(fb, fo, lsem.at[3]), pltpu.make_async_copy(sb, so, lsem.at[4])]
    for copy in outs:
        copy.start()

    def back(d, first_part):
        k = (zh + d) % 4
        s = jnp.concatenate([Sb[2 * k].reshape(512, 128), Sb[2 * k + 1].reshape(512, 128)], axis=1)
        part = jnp.dot(left(k), s, preferred_element_type=F32)
        if first_part:
            Ba[...] = part
        else:
            Ba[...] += part

    for s in (2, 3):
        for i in range(2):
            recv(("cp", s - 1, i), Sb.at[zi(9 - s), i])
            send(("cp", s, i), Sb.at[zi(9 - s), i], Sb.at[zi(9 - s), i], zn(1))
            recv(("cm", s - 1, i), Sb.at[zi(s - 1), i])
            send(("cm", s, i), Sb.at[zi(s - 1), i], Sb.at[zi(s - 1), i], zn(7))
        if s == 2:
            back(0, True)
    recv(("cp", 3, 0), Sb.at[zi(5), 0])
    send(("cp", 4, 0), Sb.at[zi(5), 0], Sb.at[zi(5), 0], zn(1))
    recv(("cm", 3, 1), Sb.at[zi(3), 1])
    send(("cm", 4, 1), Sb.at[zi(3), 1], Sb.at[zi(3), 1], zn(7))
    recv(("cp", 3, 1), Sb.at[zi(5), 1])
    recv(("cm", 3, 0), Sb.at[zi(3), 0])
    back(1, False)
    back(3, False)
    recv(("cp", 4, 0), Sb.at[zi(4), 0])
    recv(("cm", 4, 1), Sb.at[zi(4), 1])
    back(2, False)
    Bk[...] = Ba[...].astype(BF16)
    send("bk", Bk, Bs, sib)
    recv("rs0", Rs.at[zl])
    recv("rs1", Rs.at[1 - zl])
    recv("bk", Bs)

    def partial(d):
        k = (x + d) % 4
        rows = pl.ds(pl.multiple_of((k // 2) * 512, 512), 512)
        n = pl.ds((1 - k % 2) * 4, 4)
        lhs = jnp.concatenate([Bk[rows, :], Bs[rows, :]], axis=1)
        rhs = jnp.concatenate(
            [Rb[i, n, c].reshape(512, 128) for i in range(2)] + [Rs[i, n].reshape(512, 128) for i in range(2)],
            axis=1)
        res = lax.dot_general(lhs, rhs, (((1,), (1,)), ((), ())), preferred_element_type=F32).astype(BF16)
        for j in range(4):
            for h in range(2):
                Vb[k, j, h] = res[h * 256:(h + 1) * 256, j * 128:(j + 1) * 128]

    for d in (2, 1, 3):
        partial(d)
        send(("dx", d), Vb.at[(x + d) % 4, :, 1], Rd.at[1, d - 1], xn(d))
    partial(0)
    for d in (2, 1, 3):
        send(("dy", d), Vb.at[:, (y + d) % 4, 0], Rd.at[0, d - 1], yn(d))

    for d in (1, 3, 2):
        recv(("dx", d), Rd.at[1, d - 1])
    W[1] = Vb[x, :, 1].astype(F32) + Rd[1, 0].astype(F32) + Rd[1, 1].astype(F32) + Rd[1, 2].astype(F32)
    for d in (2, 1, 3):
        send(("ey", d), W.at[1, (y + d) % 4], X.at[1, d - 1], yn(d))
    for d in (1, 3, 2):
        recv(("dy", d), Rd.at[0, d - 1])
    W[0] = Vb[:, y, 0].astype(F32) + Rd[0, 0].astype(F32) + Rd[0, 1].astype(F32) + Rd[0, 2].astype(F32)
    for d in (2, 1, 3):
        send(("ex", d), W.at[0, (x + d) % 4], X.at[0, d - 1], xn(d))
    for d in (1, 3, 2):
        recv(("ey", d), X.at[1, d - 1])
    Fb[1] = W[1, y] + X[1, 0] + X[1, 1] + X[1, 2]
    send(("f", 1), Fb.at[1], upd.at[0], g_from)
    for d in (1, 3, 2):
        recv(("ex", d), X.at[0, d - 1])
    Fb[0] = W[0, x] + X[0, 0] + X[0, 1] + X[0, 2]
    send(("f", 0), Fb.at[0], upd.at[1], g_from)
    recv(("f", 1), upd.at[0])
    recv(("f", 0), upd.at[1])
    for copy in outs:
        copy.wait()
    for copy in sent:
        copy.wait_send()
    assert len(slots) <= SLOTS, len(slots)


def body(gradient, first_moment, second_moment, left_basis, right_basis):
    hbm = pl.BlockSpec(memory_space=pl.ANY)
    vm = pltpu.VMEM
    update, first_new, second_new = pl.pallas_call(
        kernel,
        out_shape=(
            jax.ShapeDtypeStruct((2, 256, 128), F32),
            jax.ShapeDtypeStruct((512, 128), F32),
            jax.ShapeDtypeStruct((512, 128), F32),
        ),
        in_specs=[hbm] * 5,
        out_specs=(hbm, hbm, hbm),
        scratch_shapes=[
            vm((4, 4, 2, 2, 256, 128), BF16),
            vm((4, 4, 2, 32, 2048), BF16),
            vm((2, 8, 2, 128, 128), BF16),
            vm((2, 8, 128, 128), BF16),
            vm((256, 1024), BF16),
            vm((8, 2, 64, 512), BF16),
            vm((4, 2, 64, 512), BF16),
            vm((4, 2, 64, 512), BF16),
            vm((8, 2, 256, 128), BF16),
            vm((1024, 256), F32),
            vm((1024, 256), BF16),
            vm((1024, 256), BF16),
            vm((4, 4, 2, 256, 128), BF16),
            vm((2, 3, 4, 256, 128), BF16),
            vm((2, 4, 256, 128), F32),
            vm((2, 3, 256, 128), F32),
            vm((2, 256, 128), F32),
            vm((512, 128), F32),
            vm((512, 128), F32),
            vm((512, 128), F32),
            vm((512, 128), F32),
            pltpu.SemaphoreType.DMA((SLOTS,)),
            pltpu.SemaphoreType.DMA((SLOTS,)),
            pltpu.SemaphoreType.DMA((5,)),
        ],
        compiler_params=pltpu.CompilerParams(
            collective_id=0, has_side_effects=True, vmem_limit_bytes=50 * 2**20),
        cost_estimate=pl.CostEstimate(flops=5 * 10**9, bytes_accessed=10**7, transcendentals=10**5),
    )(
        gradient.reshape(2, 256, 128),
        left_basis,
        right_basis.reshape(8, 2, 128, 128),
        first_moment,
        second_moment,
    )
    return update.reshape(512, 128), first_new, second_new


def solution(mesh):
    place = P("row", "col")
    placed = (place, place, place, P("col", "row"), place)
    return jax.shard_map(
        body, mesh=mesh, in_specs=placed, out_specs=(place, place, place), check_vma=False)
```

```python
import functools

import jax
import jax.numpy as jnp
from jax import lax
from jax.experimental import pallas as pl
from jax.experimental.pallas import tpu as pltpu
from jax.sharding import PartitionSpec as P

STEP = 10
beta_one = 0.9
beta_two = 0.95
epsilon = 1e-08

MESH = pl.DeviceIdType.MESH
F32 = jnp.float32
BF16 = jnp.bfloat16
SLOTS = 176


def kernel(g, l, r, m, v, upd, fo, so, Gx, Gb, Lb, Rb, Rs, Tt, Qb, Bp, Bm, Sb, Ba, Bk, Bs,
           Vb, Rd, W, X, Fb, mb, vb, fb, sb, ssem, rsem, lsem):
    zh = lax.axis_index("row")
    col = lax.axis_index("col")
    c = col % 2
    y = (col // 2) % 4
    zl = (col // 8) % 2
    x = col // 16
    z = 2 * zh + zl

    def dev(x_, y_, z_, c_):
        return (z_ // 2, ((x_ * 2 + z_ % 2) * 4 + y_) * 2 + c_)

    def xn(d):
        return dev((x + d) % 4, y, z, c)

    def yn(d):
        return dev(x, (y + d) % 4, z, c)

    def zn(d):
        return dev(x, y, (z + d) % 8, c)

    def half(k):
        return (1 + (k + 1) // 2) % 2

    sib = dev(x, y, z, 1 - c)
    pair = dev(x, y, 2 * zh + 1 - zl, c)
    b1, b0 = zh // 2, zh % 2
    g_slot = 2 * b0 + zl
    s0 = (x + 4 - zh) % 4
    mine = (zl + half(zh)) % 2
    final_to = dev(zh, y, 2 * (2 * mine + s0 // 2) + s0 % 2, c)
    final_from = dev((g_slot + x) % 4, y, 2 * x + (b1 + half(x)) % 2, c)
    xa = (x + 4 - g_slot) % 4
    z_to = 2 * xa + (b1 + half(xa)) % 2
    z_from = 2 * (2 * mine + s0 // 2) + s0 % 2
    l_slot = 2 * (x % 2) + zl
    t0 = (x + 2 - 2 * half(zh)) % 4
    l_to, l_from = [], []
    for d in range(4):
        k = (zh + d) % 4
        l_to.append(dev((l_slot + 2 - 2 * half(k)) % 4, y, 2 * k + (x // 2 + half(k)) % 2, c))
        k = (zh + 4 - d) % 4
        l_from.append(dev(2 * mine + t0 // 2, y, 2 * k + t0 % 2, c))

    slots = {}
    sent = []

    def slot(name):
        return slots.setdefault(name, len(slots))

    def send(name, src, dst, to):
        k = slot(name)
        copy = pltpu.make_async_remote_copy(
            src_ref=src, dst_ref=dst, send_sem=ssem.at[k], recv_sem=rsem.at[k],
            device_id=to, device_id_type=MESH)
        copy.start()
        sent.append(copy)

    def recv(name, dst):
        k = slot(name)
        pltpu.make_async_remote_copy(
            src_ref=dst, dst_ref=dst, send_sem=ssem.at[k], recv_sem=rsem.at[k],
            device_id=sib, device_id_type=MESH).wait_recv()

    own = [
        pltpu.make_async_copy(r, Rb.at[zl], lsem.at[0]),
        pltpu.make_async_copy(m, mb, lsem.at[1]),
        pltpu.make_async_copy(v, vb, lsem.at[2]),
    ]
    for copy in own:
        copy.start()

    barrier = pltpu.get_barrier_semaphore()
    partners = [final_to, final_from, sib, zn(1), zn(7)] + l_to + l_from
    partners += [dev(x, y, k, jnp.where(k == z, 1 - c, c)) for k in (z_to, z_from)]
    partners += [xn(d) for d in (1, 2, 3)] + [yn(d) for d in (1, 2, 3)]
    for p in partners:
        pl.semaphore_signal(barrier, inc=1, device_id=p, device_id_type=MESH)
    pl.semaphore_wait(barrier, len(partners))

    o = 1 - c
    lo, hi = pl.ds(0, 2), pl.ds(2, 2)
    full = slice(None)
    sm, sp, s2 = (s0 + 3) % 4, (s0 + 1) % 4, (s0 + 2) % 4
    tm, tp, t2 = (t0 + 3) % 4, (t0 + 1) % 4, (t0 + 2) % 4
    ym, yp, y2 = (y + 3) % 4, (y + 1) % 4, (y + 2) % 4

    def same(name, ref, to):
        send(name, ref, ref, to)

    lpos = {2: 0, 3: 512, 1: 1024, 0: 1536}
    for d in (2, 3, 1, 0):
        send(("lp", d), l, Lb.at[l_slot, y, c, :, pl.ds(lpos[d], 512)], l_to[d])
    gm = [slot(("gm", h)) for h in range(2)]

    def move(h):
        return pltpu.make_async_remote_copy(
            src_ref=g.at[h], dst_ref=Gx.at[h], send_sem=ssem.at[gm[h]], recv_sem=rsem.at[gm[h]],
            device_id=dev((x + g_slot) % 4, y, z, c), device_id_type=MESH)

    @pl.when(g_slot != 0)
    def _():
        for h in range(2):
            move(h).start()

    @pl.when(g_slot == 0)
    def _():
        for h in range(2):
            pltpu.make_async_copy(g.at[h], Gx.at[h], rsem.at[gm[h]]).start()

    send("rs0", r.at[:, o], Rs.at[zl], sib)
    gp = [slot(("gp", h)) for h in range(2)]

    def rise(h):
        return pltpu.make_async_remote_copy(
            src_ref=Gx.at[h], dst_ref=Gb.at[g_slot, y, c, h], send_sem=ssem.at[gp[h]], recv_sem=rsem.at[gp[h]],
            device_id=dev(x, y, z_to, c), device_id_type=MESH)

    for h in range(2):
        @pl.when(g_slot != 0)
        def _():
            move(h).wait_recv()

        @pl.when(g_slot == 0)
        def _():
            pltpu.make_async_copy(g.at[h], Gx.at[h], rsem.at[gm[h]]).wait()

        @pl.when(z_to != z)
        def _():
            rise(h).start()

        @pl.when(z_to == z)
        def _():
            pltpu.make_async_copy(Gx.at[h], Gb.at[g_slot, y, c, h], rsem.at[gp[h]]).start()

    def gperm(h):
        @pl.when(z_from != z)
        def _():
            pltpu.make_async_remote_copy(
                src_ref=Gx.at[h], dst_ref=Gb.at[s0, y, c, h], send_sem=ssem.at[gp[h]], recv_sem=rsem.at[gp[h]],
                device_id=sib, device_id_type=MESH).wait_recv()

        @pl.when(z_from == z)
        def _():
            pltpu.make_async_copy(Gx.at[h], Gb.at[s0, y, c, h], rsem.at[gp[h]]).wait()

    def gwait(h):
        if h == 0:
            for d in (1, 3, 2):
                recv(("gx", d), Gb.at[(s0 + 4 - d) % 4, y, c, 0])
        else:
            for d in (1, 3, 2):
                recv(("gy", d), Gb.at[s0, (y + 4 - d) % 4, c, 1])

    lcols = {}
    for j, (at, n) in enumerate(((0, 512), (512, 1024), (1536, 512))):
        lcols[j] = (pl.ds(at, n // 2), pl.ds(at + n // 2, n // 2))

    def lp_(j, h, a, b, core=c):
        return Lb.at[a, b, core, :, lcols[j][h]]

    def lsmall(j):
        for d in (2, 1, 3):
            same(("lx", j, d), lp_(j, 0, t0, y), xn(d))
            same(("ly", j, d), lp_(j, 1, t0, y), yn(d))

    def lbig(j):
        for d in (1, 3, 2):
            recv(("lx", j, d), lp_(j, 0, (t0 + 4 - d) % 4, y))
        same(("Ly1a", j), lp_(j, 0, lo, y), yn(1))
        same(("Ly3b", j), lp_(j, 0, hi, y), yn(3))
        same(("Ly1b", j), lp_(j, 0, hi, y), yn(1))
        same(("Ly3a", j), lp_(j, 0, lo, y), yn(3))
        same(("Ls", j, 0), lp_(j, 0, full, y), sib)
        for d in (1, 3, 2):
            recv(("ly", j, d), lp_(j, 1, t0, (y + 4 - d) % 4))
        same(("Lx1a", j), lp_(j, 1, t0, lo), xn(1))
        same(("Lx3b", j), lp_(j, 1, t0, hi), xn(3))
        same(("Lx1b", j), lp_(j, 1, t0, hi), xn(1))
        same(("Lx3a", j), lp_(j, 1, t0, lo), xn(3))
        same(("Ls", j, 1), lp_(j, 1, t0, full), sib)

    def lfwd(j):
        recv(("Ly1a", j), lp_(j, 0, lo, ym))
        same(("Lyfa", j), lp_(j, 0, lo, ym), yn(1))
        recv(("Ly3b", j), lp_(j, 0, hi, yp))
        same(("Lyfb", j), lp_(j, 0, hi, yp), yn(3))
        recv(("Lx1a", j), lp_(j, 1, tm, lo))
        same(("Lxfa", j), lp_(j, 1, tm, lo), xn(1))
        recv(("Lx3b", j), lp_(j, 1, tp, hi))
        same(("Lxfb", j), lp_(j, 1, tp, hi), xn(3))

    def lshare(j):
        recv(("Ly1b", j), lp_(j, 0, hi, ym))
        same(("Ls", j, 2), lp_(j, 0, full, ym), sib)
        recv(("Ly3a", j), lp_(j, 0, lo, yp))
        same(("Ls", j, 3), lp_(j, 0, full, yp), sib)
        recv(("Lx1b", j), lp_(j, 1, tm, hi))
        same(("Ls", j, 4), lp_(j, 1, tm, full), sib)
        recv(("Lx3a", j), lp_(j, 1, tp, lo))
        same(("Ls", j, 5), lp_(j, 1, tp, full), sib)
        recv(("Lyfa", j), lp_(j, 0, lo, y2))
        recv(("Lyfb", j), lp_(j, 0, hi, y2))
        same(("Ls", j, 6), lp_(j, 0, full, y2), sib)
        recv(("Lxfa", j), lp_(j, 1, t2, lo))
        recv(("Lxfb", j), lp_(j, 1, t2, hi))
        same(("Ls", j, 7), lp_(j, 1, t2, full), sib)

    def lwait(j):
        for i, b in ((0, y), (2, ym), (3, yp), (6, y2)):
            recv(("Ls", j, i), lp_(j, 0, full, b, o))
        for i, a in ((1, t0), (4, tm), (5, tp), (7, t2)):
            recv(("Ls", j, i), lp_(j, 1, a, full, o))

    def lperm(d):
        recv(("lp", d), Lb.at[t0, y, c, :, pl.ds(lpos[d], 512)])

    for d in (2, 3, 1, 0):
        lperm(d)
    for j in range(3):
        lsmall(j)
    @pl.when(z_to != z)
    def _():
        for h in range(2):
            rise(h).wait_send()

    send("rp", r, Rb.at[zl], pair)
    gperm(0)
    for d in (2, 1, 3):
        same(("gx", d), Gb.at[s0, y, c, 0], xn(d))
    gperm(1)
    for d in (2, 1, 3):
        same(("gy", d), Gb.at[s0, y, c, 1], yn(d))
    lbig(0)

    gwait(0)
    same("Gy1a", Gb.at[lo, y, c, 0], yn(1))
    same("Gy3b", Gb.at[hi, y, c, 0], yn(3))
    same("Gy1b", Gb.at[hi, y, c, 0], yn(1))
    same("Gy3a", Gb.at[lo, y, c, 0], yn(3))
    same("Gs0", Gb.at[:, y, c, 0], sib)
    gwait(1)
    same("Gx1a", Gb.at[s0, lo, c, 1], xn(1))
    same("Gx3b", Gb.at[s0, hi, c, 1], xn(3))
    same("Gx1b", Gb.at[s0, hi, c, 1], xn(1))
    same("Gx3a", Gb.at[s0, lo, c, 1], xn(3))
    same("Gs1", Gb.at[s0, :, c, 1], sib)

    lfwd(0)
    recv("Gy1a", Gb.at[lo, ym, c, 0])
    same("Gyfa", Gb.at[lo, ym, c, 0], yn(1))
    recv("Gy3b", Gb.at[hi, yp, c, 0])
    same("Gyfb", Gb.at[hi, yp, c, 0], yn(3))
    recv("Gx1a", Gb.at[sm, lo, c, 1])
    same("Gxfa", Gb.at[sm, lo, c, 1], xn(1))
    recv("Gx3b", Gb.at[sp, hi, c, 1])
    same("Gxfb", Gb.at[sp, hi, c, 1], xn(3))
    lshare(0)
    recv("Gy1b", Gb.at[hi, ym, c, 0])
    same("Gs2", Gb.at[:, ym, c, 0], sib)
    recv("Gy3a", Gb.at[lo, yp, c, 0])
    same("Gs3", Gb.at[:, yp, c, 0], sib)
    recv("Gx1b", Gb.at[sm, hi, c, 1])
    same("Gs4", Gb.at[sm, :, c, 1], sib)
    recv("Gx3a", Gb.at[sp, lo, c, 1])
    same("Gs5", Gb.at[sp, :, c, 1], sib)
    recv("Gyfa", Gb.at[lo, y2, c, 0])
    recv("Gyfb", Gb.at[hi, y2, c, 0])
    same("Gs6", Gb.at[:, y2, c, 0], sib)
    recv("Gxfa", Gb.at[s2, lo, c, 1])
    recv("Gxfb", Gb.at[s2, hi, c, 1])
    same("Gs7", Gb.at[s2, :, c, 1], sib)
    recv("rp", Rb.at[1 - zl])
    send("rs1", Rb.at[1 - zl, :, o], Rs.at[1 - zl], sib)
    lbig(1)

    own[0].wait()
    def turn(b, h):
        lhs = jnp.concatenate(
            [Gb[2 * b + i, j, k, h] for i in range(2) for j in range(4) for k in range(2)], axis=1)
        rhs = jnp.concatenate([Rb[i].reshape(2048, 128) for i in range(2)], axis=1)
        t = jnp.dot(lhs, rhs, preferred_element_type=F32)
        q = 2 * b + h
        Tt[:, q * 256:(q + 1) * 256] = t.T.astype(BF16)

    recv("Gs0", Gb.at[:, y, o, 0])
    recv("Gs2", Gb.at[:, ym, o, 0])
    recv("Gs3", Gb.at[:, yp, o, 0])
    recv("Gs6", Gb.at[:, y2, o, 0])
    turn(0, 0)
    turn(1, 0)
    recv("Gs1", Gb.at[s0, :, o, 1])
    recv("Gs4", Gb.at[sm, :, o, 1])
    recv("Gs5", Gb.at[sp, :, o, 1])
    recv("Gs7", Gb.at[s2, :, o, 1])
    turn(0, 1)
    turn(1, 1)

    lwait(0)

    def left(d):
        at = {2: 0, 1: 512, 3: 1024, 0: 1536}[d]
        return Lb[:, :, :, :, at:at + 512].reshape(1024, 512)

    def rotate(d):
        k = (zh + d) % 4
        q = jnp.dot(Tt[...], left(d), preferred_element_type=F32)
        Qb[2 * k, 0] = q[0:64].astype(BF16)
        Qb[2 * k, 1] = q[64:128].astype(BF16)
        Qb[2 * k + 1, 0] = q[128:192].astype(BF16)
        Qb[2 * k + 1, 1] = q[192:256].astype(BF16)

    def zi(d):
        return (z + d) % 8

    rotate(2)
    send(("bp", 1, 0), Qb.at[zi(4), 0], Bp.at[0, 0], zn(1))
    send(("bm", 1, 1), Qb.at[zi(4), 1], Bm.at[0, 1], zn(7))
    lfwd(1)
    lbig(2)
    lshare(1)
    lwait(1)
    rotate(1)
    rotate(3)
    send(("bp", 2, 1), Qb.at[zi(3), 1], Bp.at[1, 1], zn(1))
    send(("bm", 2, 0), Qb.at[zi(5), 0], Bm.at[1, 0], zn(7))

    def add(k, i, buf, s):
        Qb[k, i] = (Qb[k, i].astype(F32) + buf[s, i].astype(F32)).astype(BF16)

    for s, order in ((2, (0,)), (3, (1, 0)), (4, (1, 0))):
        for i in order:
            j = i
            recv(("bp", s - 1, j), Bp.at[s - 2, j])
            add(zi(5 - s), j, Bp, s - 2)
            send(("bp", s, j), Qb.at[zi(5 - s), j], Bp.at[s - 1, j], zn(1))
            j = 1 - i
            recv(("bm", s - 1, j), Bm.at[s - 2, j])
            add(zi(3 + s), j, Bm, s - 2)
            send(("bm", s, j), Qb.at[zi(3 + s), j], Bm.at[s - 1, j], zn(7))
        if s == 2:
            lfwd(2)
        if s == 3:
            lshare(2)
            lwait(2)
            rotate(0)
    own[1].wait()
    own[2].wait()
    for i in range(2):
        recv(("bp", 4, i), Bp.at[3, i])
        recv(("bm", 4, i), Bm.at[3, i])
    total = Qb[z].reshape(128, 512).astype(F32) + Bp[3].reshape(128, 512).astype(F32) \
        + Bm[3].reshape(128, 512).astype(F32)
    rotated = total.T
    first = beta_one * mb[...] + (1.0 - beta_one) * rotated
    second = beta_two * vb[...] + (1.0 - beta_two) * rotated * rotated
    one = first * (1.0 / (1.0 - beta_one**STEP))
    two = second * (1.0 / (1.0 - beta_two**STEP))
    scaled = (one / (jnp.sqrt(two) + epsilon)).astype(BF16)
    Sb[z, 0] = scaled[0:256]
    Sb[z, 1] = scaled[256:512]
    for i in range(2):
        send(("cp", 1, i), Sb.at[z, i], Sb.at[z, i], zn(1))
        send(("cm", 1, i), Sb.at[z, i], Sb.at[z, i], zn(7))
    fb[...] = first
    sb[...] = second
    outs = [pltpu.make_async_copy(fb, fo, lsem.at[3]), pltpu.make_async_copy(sb, so, lsem.at[4])]
    for copy in outs:
        copy.start()

    def back(d, first_part):
        k = (zh + d) % 4
        s = jnp.concatenate([Sb[2 * k].reshape(512, 128), Sb[2 * k + 1].reshape(512, 128)], axis=1)
        part = jnp.dot(left(d), s, preferred_element_type=F32)
        if first_part:
            Ba[...] = part
        else:
            Ba[...] += part

    for s in (2, 3):
        for i in range(2):
            recv(("cp", s - 1, i), Sb.at[zi(9 - s), i])
            send(("cp", s, i), Sb.at[zi(9 - s), i], Sb.at[zi(9 - s), i], zn(1))
            recv(("cm", s - 1, i), Sb.at[zi(s - 1), i])
            send(("cm", s, i), Sb.at[zi(s - 1), i], Sb.at[zi(s - 1), i], zn(7))
        if s == 2:
            back(0, True)
    recv(("cp", 3, 0), Sb.at[zi(5), 0])
    send(("cp", 4, 0), Sb.at[zi(5), 0], Sb.at[zi(5), 0], zn(1))
    recv(("cm", 3, 1), Sb.at[zi(3), 1])
    send(("cm", 4, 1), Sb.at[zi(3), 1], Sb.at[zi(3), 1], zn(7))
    recv(("cp", 3, 1), Sb.at[zi(5), 1])
    recv(("cm", 3, 0), Sb.at[zi(3), 0])
    back(1, False)
    back(3, False)
    recv(("cp", 4, 0), Sb.at[zi(4), 0])
    recv(("cm", 4, 1), Sb.at[zi(4), 1])
    back(2, False)
    Bk[...] = Ba[...].astype(BF16)
    send("bk", Bk, Bs, sib)
    recv("rs0", Rs.at[zl])
    recv("rs1", Rs.at[1 - zl])
    recv("bk", Bs)

    def partial(k, u):
        rows = [pl.ds(pl.multiple_of((k // 2) * 512 + h * 256 + u * 128, 128), 128) for h in range(2)]
        n = pl.ds((k % 2) * 4, 4)
        lhs = jnp.concatenate(
            [jnp.concatenate([Bk[i, :], Bs[i, :]], axis=1) for i in rows], axis=0)
        rhs = jnp.concatenate(
            [Rb[i, n, c].reshape(512, 128) for i in range(2)] + [Rs[i, n].reshape(512, 128) for i in range(2)],
            axis=1)
        res = lax.dot_general(lhs, rhs, (((1,), (1,)), ((), ())), preferred_element_type=F32).astype(BF16)
        for j in range(4):
            for h in range(2):
                Vb[k, j, h, u] = res[h * 128:(h + 1) * 128, j * 128:(j + 1) * 128]

    for u in range(2):
        for d in (2, 1, 3):
            partial((s0 + d) % 4, u)
            send(("dx", d, u), Vb.at[(s0 + d) % 4, :, 1, u], Rd.at[1, u, d - 1], xn(d))
        partial(s0, u)
        for d in (2, 1, 3):
            send(("dy", d, u), Vb.at[:, (y + d) % 4, 0, u], Rd.at[0, u, d - 1], yn(d))

    def gather_sum(u):
        for d in (1, 3, 2):
            recv(("dx", d, u), Rd.at[1, u, d - 1])
        W[1, u] = Vb[s0, :, 1, u].astype(F32) + Rd[1, u, 0].astype(F32) + Rd[1, u, 1].astype(F32) \
            + Rd[1, u, 2].astype(F32)
        for d in (2, 1, 3):
            send(("ey", d, u), W.at[1, u, (y + d) % 4], X.at[1, u, d - 1], yn(d))
        for d in (1, 3, 2):
            recv(("dy", d, u), Rd.at[0, u, d - 1])
        W[0, u] = Vb[:, y, 0, u].astype(F32) + Rd[0, u, 0].astype(F32) + Rd[0, u, 1].astype(F32) \
            + Rd[0, u, 2].astype(F32)
        for d in (2, 1, 3):
            send(("ex", d, u), W.at[0, u, (s0 + d) % 4], X.at[0, u, d - 1], xn(d))

    def final_sum(u):
        for d in (1, 3, 2):
            recv(("ey", d, u), X.at[1, u, d - 1])
        Fb[1, u] = W[1, u, y] + X[1, u, 0] + X[1, u, 1] + X[1, u, 2]
        send(("f", 1, u), Fb.at[1, u], upd.at[1, u], final_to)
        for d in (1, 3, 2):
            recv(("ex", d, u), X.at[0, u, d - 1])
        Fb[0, u] = W[0, u, s0] + X[0, u, 0] + X[0, u, 1] + X[0, u, 2]
        send(("f", 0, u), Fb.at[0, u], upd.at[0, u], final_to)

    gather_sum(0)
    gather_sum(1)
    final_sum(0)
    final_sum(1)
    for u in range(2):
        recv(("f", 1, u), upd.at[1, u])
        recv(("f", 0, u), upd.at[0, u])
    for copy in outs:
        copy.wait()
    @pl.when(g_slot != 0)
    def _():
        for h in range(2):
            move(h).wait_send()

    for copy in sent:
        copy.wait_send()
    assert len(slots) <= SLOTS, len(slots)


def body(gradient, first_moment, second_moment, left_basis, right_basis):
    hbm = pl.BlockSpec(memory_space=pl.ANY)
    vm = pltpu.VMEM
    update, first_new, second_new = pl.pallas_call(
        kernel,
        out_shape=(
            jax.ShapeDtypeStruct((2, 2, 128, 128), F32),
            jax.ShapeDtypeStruct((512, 128), F32),
            jax.ShapeDtypeStruct((512, 128), F32),
        ),
        in_specs=[hbm] * 5,
        out_specs=(hbm, hbm, hbm),
        scratch_shapes=[
            vm((2, 256, 128), BF16),
            vm((4, 4, 2, 2, 256, 128), BF16),
            vm((4, 4, 2, 32, 2048), BF16),
            vm((2, 8, 2, 128, 128), BF16),
            vm((2, 8, 128, 128), BF16),
            vm((256, 1024), BF16),
            vm((8, 2, 64, 512), BF16),
            vm((4, 2, 64, 512), BF16),
            vm((4, 2, 64, 512), BF16),
            vm((8, 2, 256, 128), BF16),
            vm((1024, 256), F32),
            vm((1024, 256), BF16),
            vm((1024, 256), BF16),
            vm((4, 4, 2, 2, 128, 128), BF16),
            vm((2, 2, 3, 4, 128, 128), BF16),
            vm((2, 2, 4, 128, 128), F32),
            vm((2, 2, 3, 128, 128), F32),
            vm((2, 2, 128, 128), F32),
            vm((512, 128), F32),
            vm((512, 128), F32),
            vm((512, 128), F32),
            vm((512, 128), F32),
            pltpu.SemaphoreType.DMA((SLOTS,)),
            pltpu.SemaphoreType.DMA((SLOTS,)),
            pltpu.SemaphoreType.DMA((5,)),
        ],
        compiler_params=pltpu.CompilerParams(
            collective_id=0, has_side_effects=True, vmem_limit_bytes=63 * 2**20),
        cost_estimate=pl.CostEstimate(flops=5 * 10**9, bytes_accessed=10**7, transcendentals=10**5),
    )(
        gradient.reshape(2, 256, 128),
        left_basis,
        right_basis.reshape(8, 2, 128, 128),
        first_moment,
        second_moment,
    )
    return update.reshape(512, 128), first_new, second_new


def solution(mesh):
    place = P("row", "col")
    placed = (place, place, place, P("col", "row"), place)
    return jax.shard_map(
        body, mesh=mesh, in_specs=placed, out_specs=(place, place, place), check_vma=False)
```

```python
import math

import jax
import jax.numpy as jnp
from jax import lax
from jax.experimental import pallas as pl
from jax.experimental.pallas import tpu as pltpu
from jax.sharding import PartitionSpec as P

STEP = 10
beta_one = 0.9
beta_two = 0.95
epsilon = 1e-08

MESH = pl.DeviceIdType.MESH
F32 = jnp.float32
BF16 = jnp.bfloat16
SLOTS = 160


def kernel(g, l, r, m, v, upd, fo, so, Gx, Gb, Lb, Rb, Rs, Tt, Qf, Qs, Bp, Bm, Sb, So, Ba, Bk,
           Vb, Ra, Rd, W, Wb, X, Fb, mb, vb, fb, sb, ssem, rsem, lsem, msem):
    zh = lax.axis_index("row")
    col = lax.axis_index("col")
    c = col % 2
    y = (col // 2) % 4
    zl = (col // 8) % 2
    x = col // 16
    z = 2 * zh + zl

    def dev(x_, y_, z_, c_):
        return (z_ // 2, ((x_ * 2 + z_ % 2) * 4 + y_) * 2 + c_)

    def xn(d):
        return dev((x + d) % 4, y, z, c)

    def yn(d):
        return dev(x, (y + d) % 4, z, c)

    def zn(d):
        return dev(x, y, (z + d) % 8, c)

    def half(k):
        return (1 + (k + 1) // 2) % 2

    sib = dev(x, y, z, 1 - c)
    pair = dev(x, y, 2 * zh + 1 - zl, c)
    b1, b0 = zh // 2, zh % 2
    g_slot = 2 * b0 + zl
    s0 = (x + 4 - zh) % 4
    mine = (zl + half(zh)) % 2
    final_to = dev(zh, y, 2 * (2 * mine + s0 // 2) + s0 % 2, c)
    final_from = dev((g_slot + x) % 4, y, 2 * x + (b1 + half(x)) % 2, c)
    xa = (x + 4 - g_slot) % 4
    z_to = 2 * xa + (b1 + half(xa)) % 2
    z_from = 2 * (2 * mine + s0 // 2) + s0 % 2
    l_slot = 2 * (x % 2) + zl
    t0 = (x + 2 - 2 * half(zh)) % 4
    l_to, l_from = [], []
    for d in range(4):
        k = (zh + d) % 4
        l_to.append(dev((l_slot + 2 - 2 * half(k)) % 4, y, 2 * k + (x // 2 + half(k)) % 2, c))
        k = (zh + 4 - d) % 4
        l_from.append(dev(2 * mine + t0 // 2, y, 2 * k + t0 % 2, c))

    slots = {}
    sent = []

    def slot(name):
        return slots.setdefault(name, len(slots))

    def begin():
        sent.append(0)

    def send(name, src, dst, to):
        k = slot(name)
        pltpu.make_async_remote_copy(
            src_ref=src, dst_ref=dst, send_sem=ssem.at[len(sent) - 1], recv_sem=rsem.at[k],
            device_id=to, device_id_type=MESH).start()
        sent[-1] += math.prod(dst.shape) * dst.dtype.itemsize

    def recv(name, dst):
        pltpu.make_async_remote_copy(
            src_ref=dst, dst_ref=dst, send_sem=ssem.at[0], recv_sem=rsem.at[slot(name)],
            device_id=sib, device_id_type=MESH).wait_recv()

    def left_device(phase):
        rest = sent[phase]
        for unit, ref in ((2**20, Gb), (2**18, Gb.at[0]), (2**17, Gb.at[0, 0]), (2**16, Gb.at[0, 0, 0]),
                          (2**12, Gb.at[0, 0, 0, 0])):
            n, rest = rest // unit, rest % unit
            while n > 0:
                now = min(n, ref.shape[0] if unit > 2**12 else 16)
                part = ref.at[pl.ds(0, now if unit > 2**12 else 16 * now)]
                pltpu.make_async_remote_copy(
                    src_ref=part, dst_ref=part, send_sem=ssem.at[phase], recv_sem=rsem.at[0],
                    device_id=sib, device_id_type=MESH).wait_send()
                n -= now
        assert rest == 0

    begin()
    own = [
        pltpu.make_async_copy(r, Rb.at[zl], lsem.at[0]),
        pltpu.make_async_copy(m, mb, lsem.at[1]),
        pltpu.make_async_copy(v, vb, lsem.at[2]),
    ]
    for copy in own:
        copy.start()

    barrier = pltpu.get_barrier_semaphore()
    partners = [final_to, final_from, sib, zn(1), zn(7)] + l_to + l_from
    partners += [dev(x, y, k, jnp.where(k == z, 1 - c, c)) for k in (z_to, z_from)]
    partners += [xn(d) for d in (1, 2, 3)] + [yn(d) for d in (1, 2, 3)]
    for p in partners:
        pl.semaphore_signal(barrier, inc=1, device_id=p, device_id_type=MESH)
    pl.semaphore_wait(barrier, len(partners))

    o = 1 - c
    lo, hi = pl.ds(0, 2), pl.ds(2, 2)
    full = slice(None)
    sm, sp, s2 = (s0 + 3) % 4, (s0 + 1) % 4, (s0 + 2) % 4
    tm, tp, t2 = (t0 + 3) % 4, (t0 + 1) % 4, (t0 + 2) % 4
    ym, yp, y2 = (y + 3) % 4, (y + 1) % 4, (y + 2) % 4

    def same(name, ref, to):
        send(name, ref, ref, to)

    def lplace(rel, low):
        return {2: 0, 0: 3}.get(rel, 1 + low if rel == 1 else 2 - low)

    for d in (2, 3, 1, 0):
        low = (x // 2 + half((zh + d) % 4)) % 2
        for h in range(2):
            send(("lp", d), l.at[:, pl.ds(h * 256, 256)], Lb.at[l_slot, y, c, lplace((4 - d) % 4, low), h], l_to[d])
    gm = [slot(("gm", h)) for h in range(2)]

    def move(h):
        return pltpu.make_async_remote_copy(
            src_ref=g.at[h], dst_ref=Gx.at[h], send_sem=msem.at[h], recv_sem=rsem.at[gm[h]],
            device_id=dev((x + g_slot) % 4, y, z, c), device_id_type=MESH)

    @pl.when(g_slot != 0)
    def _():
        for h in range(2):
            move(h).start()

    @pl.when(g_slot == 0)
    def _():
        for h in range(2):
            pltpu.make_async_copy(g.at[h], Gx.at[h], rsem.at[gm[h]]).start()

    send("rs0", r.at[:, o], Rs.at[zl], sib)
    gp = [slot(("gp", h)) for h in range(2)]

    def rise(h):
        return pltpu.make_async_remote_copy(
            src_ref=Gx.at[h], dst_ref=Gb.at[g_slot, y, c, h], send_sem=msem.at[2 + h], recv_sem=rsem.at[gp[h]],
            device_id=dev(x, y, z_to, c), device_id_type=MESH)

    for h in range(2):
        @pl.when(g_slot != 0)
        def _():
            move(h).wait_recv()

        @pl.when(g_slot == 0)
        def _():
            pltpu.make_async_copy(g.at[h], Gx.at[h], rsem.at[gm[h]]).wait()

        @pl.when(z_to != z)
        def _():
            rise(h).start()

        @pl.when(z_to == z)
        def _():
            pltpu.make_async_copy(Gx.at[h], Gb.at[g_slot, y, c, h], rsem.at[gp[h]]).start()

    def gperm(h):
        @pl.when(z_from != z)
        def _():
            pltpu.make_async_remote_copy(
                src_ref=Gx.at[h], dst_ref=Gb.at[s0, y, c, h], send_sem=msem.at[2 + h], recv_sem=rsem.at[gp[h]],
                device_id=sib, device_id_type=MESH).wait_recv()

        @pl.when(z_from == z)
        def _():
            pltpu.make_async_copy(Gx.at[h], Gb.at[s0, y, c, h], rsem.at[gp[h]]).wait()

    lcols = (pl.ds(0, 1), pl.ds(1, 2), pl.ds(3, 1))

    def lp_(j, h, a, b):
        return Lb.at[a, b, c, lcols[j], h]

    for d in (2, 3, 1, 0):
        recv(("lp", d), Lb.at[t0, y, c, lplace((4 - d) % 4, zl)])
    for d in (2, 1, 3):
        same("lx", Lb.at[t0, y, c, :, 0], xn(d))
        same("ly", Lb.at[t0, y, c, :, 1], yn(d))

    def lbig(j):
        for d in (1, 3):
            same(("Ly", d, j), lp_(j, 0, full, y), yn(d))
            same(("Lx", d, j), lp_(j, 1, t0, full), xn(d))

    def lfwd(j):
        recv(("Ly", 1, j), lp_(j, 0, full, ym))
        same(("Lyf", j), lp_(j, 0, lo, ym), yn(1))
        recv(("Ly", 3, j), lp_(j, 0, full, yp))
        same(("Lyf", j), lp_(j, 0, hi, yp), yn(3))
        recv(("Lx", 1, j), lp_(j, 1, tm, full))
        same(("Lxf", j), lp_(j, 1, tm, lo), xn(1))
        recv(("Lx", 3, j), lp_(j, 1, tp, full))
        same(("Lxf", j), lp_(j, 1, tp, hi), xn(3))

    def lshare(j):
        recv(("Lyf", j), lp_(j, 0, full, y2))
        recv(("Lxf", j), lp_(j, 1, t2, full))
        for i in {0: (0,), 1: (1, 2), 2: (3,)}[j]:
            same(("Ls", i), Lb.at[:, :, c, i], sib)

    def lwait(i):
        recv(("Ls", i), Lb.at[:, :, o, i])

    @pl.when(z_to != z)
    def _():
        for h in range(2):
            rise(h).wait_send()

    send("rp", r, Rb.at[zl], pair)
    three = pl.ds(0, 3)
    gperm(0)
    for d in (2, 1, 3):
        same("gx", Gb.at[s0, y, c, 0], xn(d))
    gperm(1)
    for d in (2, 1, 3):
        same("gy", Gb.at[s0, y, c, 1], yn(d))
    recv("lx", Lb.at[three, y, c, :, 0])
    recv("ly", Lb.at[t0, three, c, :, 1])
    lbig(0)

    recv("gx", Gb.at[three, y, c, 0])
    same("Gy1a", Gb.at[lo, y, c, 0], yn(1))
    same("Gy3b", Gb.at[hi, y, c, 0], yn(3))
    same("Gy1b", Gb.at[hi, y, c, 0], yn(1))
    same("Gy3a", Gb.at[lo, y, c, 0], yn(3))
    recv("gy", Gb.at[s0, three, c, 1])
    same("Gx1a", Gb.at[s0, lo, c, 1], xn(1))
    same("Gx3b", Gb.at[s0, hi, c, 1], xn(3))
    same("Gx1b", Gb.at[s0, hi, c, 1], xn(1))
    same("Gx3a", Gb.at[s0, lo, c, 1], xn(3))
    same("Gs0", Gb.at[:, y, c, 0], sib)
    same("Gs1", Gb.at[s0, :, c, 1], sib)
    lfwd(0)
    recv("Gy1a", Gb.at[lo, ym, c, 0])
    same("Gyf", Gb.at[lo, ym, c, 0], yn(1))
    recv("Gy3b", Gb.at[hi, yp, c, 0])
    same("Gyf", Gb.at[hi, yp, c, 0], yn(3))
    recv("Gx1a", Gb.at[sm, lo, c, 1])
    same("Gxf", Gb.at[sm, lo, c, 1], xn(1))
    recv("Gx3b", Gb.at[sp, hi, c, 1])
    same("Gxf", Gb.at[sp, hi, c, 1], xn(3))
    lbig(1)
    recv("Gy1b", Gb.at[hi, ym, c, 0])
    same("Gs0", Gb.at[:, ym, c, 0], sib)
    recv("Gy3a", Gb.at[lo, yp, c, 0])
    same("Gs0", Gb.at[:, yp, c, 0], sib)
    recv("Gx1b", Gb.at[sm, hi, c, 1])
    same("Gs1", Gb.at[sm, :, c, 1], sib)
    recv("Gx3a", Gb.at[sp, lo, c, 1])
    same("Gs1", Gb.at[sp, :, c, 1], sib)
    recv("Gyf", Gb.at[:, y2, c, 0])
    same("Gs0", Gb.at[:, y2, c, 0], sib)
    recv("Gxf", Gb.at[s2, :, c, 1])
    same("Gs1", Gb.at[s2, :, c, 1], sib)
    lshare(0)
    recv("rp", Rb.at[1 - zl])
    send("rs1", Rb.at[1 - zl, :, o], Rs.at[1 - zl], sib)

    own[0].wait()
    def turn(b, h):
        lhs = jnp.concatenate(
            [Gb[2 * b + i, j, k, h] for i in range(2) for j in range(4) for k in range(2)], axis=1)
        rhs = jnp.concatenate([Rb[i].reshape(2048, 128) for i in range(2)], axis=1)
        t = jnp.dot(lhs, rhs, preferred_element_type=F32)
        q = 2 * b + h
        Tt[:, q * 256:(q + 1) * 256] = t.T.astype(BF16)

    recv("Gs0", Gb.at[:, :, o, 0])
    turn(0, 0)
    turn(1, 0)
    lfwd(1)
    recv("Gs1", Gb.at[:, :, o, 1])
    turn(0, 1)
    turn(1, 1)

    lwait(0)

    def left(j):
        return jnp.concatenate([Lb[:, :, :, j, h].reshape(1024, 256) for h in range(2)], axis=1)

    rels = (2, 1 + 2 * zl, 3 - 2 * zl, 0)

    def rotate(p):
        k = (zh + rels[p]) % 4
        q = jnp.dot(Tt[...], left(p), preferred_element_type=F32)
        for i in range(2):
            for j in range(2):
                part = q[i * 128:(i + 1) * 128, j * 256:(j + 1) * 256]
                Qf[2 * k + i, j] = part
                Qs[2 * k + i, j] = part.astype(BF16)

    def zi(d):
        return (z + d) % 8

    ha, hb = pl.ds(0, 64), pl.ds(64, 64)
    rotate(0)
    for j in range(2):
        send(("bp", 1, j), Qs.at[zi(4), j, ha], Bp.at[0, j, ha], zn(1))
        send(("bm", 1, j), Qs.at[zi(4), j, hb], Bm.at[0, j, hb], zn(7))
    lshare(1)
    lbig(2)
    lwait(1)
    rotate(1)
    send("bpe", Qs.at[zi(3), :, hb], Bp.at[1, :, hb], zn(1))
    send("bme", Qs.at[zi(5), :, ha], Bm.at[1, :, ha], zn(7))

    for j in range(2):
        k = zi(3)
        recv(("bp", 1, j), Bp.at[0, j, ha])
        Qs[k, j, ha] = (Qf[k, j, ha] + Bp[0, j, ha].astype(F32)).astype(BF16)
        send(("bp", 2, j), Qs.at[k, j, ha], Bp.at[1, j, ha], zn(1))
        k = zi(5)
        recv(("bm", 1, j), Bm.at[0, j, hb])
        Qs[k, j, hb] = (Qf[k, j, hb] + Bm[0, j, hb].astype(F32)).astype(BF16)
        send(("bm", 2, j), Qs.at[k, j, hb], Bm.at[1, j, hb], zn(7))
    lwait(2)
    rotate(2)
    lfwd(2)
    recv("bpe", Bp.at[1, :, hb])
    recv("bme", Bm.at[1, :, ha])
    for s in (3, 4):
        for j in range(2):
            k = zi(5 - s)
            recv(("bp", s - 1, j), Bp.at[s - 2, j] if s > 3 else Bp.at[1, j, ha])
            Qs[k, j] = (Qf[k, j] + Bp[s - 2, j].astype(F32)).astype(BF16)
            send(("bp", s, j), Qs.at[k, j], Bp.at[s - 1, j], zn(1))
            k = zi(3 + s)
            recv(("bm", s - 1, j), Bm.at[s - 2, j] if s > 3 else Bm.at[1, j, hb])
            Qs[k, j] = (Qf[k, j] + Bm[s - 2, j].astype(F32)).astype(BF16)
            send(("bm", s, j), Qs.at[k, j], Bm.at[s - 1, j], zn(7))
        if s == 3:
            lshare(2)
            lwait(3)
            rotate(3)
    own[1].wait()
    own[2].wait()
    begin()
    for j in range(2):
        recv(("bp", 4, j), Bp.at[3, j])
        recv(("bm", 4, j), Bm.at[3, j])
        rows = slice(j * 256, (j + 1) * 256)
        rotated = (Qf[z, j] + Bp[3, j].astype(F32) + Bm[3, j].astype(F32)).T
        first = beta_one * mb[rows] + (1.0 - beta_one) * rotated
        second = beta_two * vb[rows] + (1.0 - beta_two) * rotated * rotated
        one = first * (1.0 / (1.0 - beta_one**STEP))
        two = second * (1.0 / (1.0 - beta_two**STEP))
        scaled = (one / (jnp.sqrt(two) + epsilon)).astype(BF16)
        for i in (2 * j, 2 * j + 1):
            Sb[z, i] = scaled[(i - 2 * j) * 128:(i - 2 * j + 1) * 128]
            same(("cp", 1, i), Sb.at[z, i], zn(1))
            same(("cm", 1, i), Sb.at[z, i], zn(7))
        fb[rows] = first
        sb[rows] = second
    outs = [pltpu.make_async_copy(fb, fo, lsem.at[3]), pltpu.make_async_copy(sb, so, lsem.at[4])]
    for copy in outs:
        copy.start()

    left_device(0)
    def across(d):
        send(("ss", d), Sb.at[zi(d)], So.at[zi(d)], sib)

    def crossed(*ds):
        for d in ds:
            recv(("ss", d), So.at[zi(d)])

    def back(j, first_part):
        k = (zh + rels[j]) % 4
        s = jnp.concatenate(
            [ref[2 * k + i].reshape(512, 128) for ref in (Sb, So) for i in range(2)], axis=1)
        part = jnp.dot(left(j), s, preferred_element_type=F32)
        if first_part:
            Ba[...] = part
        else:
            Ba[...] += part

    across(0)
    for s in (2, 3):
        for j in range(4):
            recv(("cp", s - 1, j), Sb.at[zi(9 - s), j])
            same(("cp", s, j), Sb.at[zi(9 - s), j], zn(1))
            recv(("cm", s - 1, j), Sb.at[zi(s - 1), j])
            same(("cm", s, j), Sb.at[zi(s - 1), j], zn(7))
        across(9 - s)
        across(s - 1)
    crossed(0, 1, 7)
    back(3, True)
    for j in range(2):
        recv(("cp", 3, j), Sb.at[zi(5), j])
        same(("cp", 4, j), Sb.at[zi(5), j], zn(1))
        recv(("cm", 3, j + 2), Sb.at[zi(3), j + 2])
        same(("cm", 4, j + 2), Sb.at[zi(3), j + 2], zn(7))
    for j in range(2):
        recv(("cp", 3, j + 2), Sb.at[zi(5), j + 2])
        recv(("cm", 3, j), Sb.at[zi(3), j])
    across(5)
    across(3)
    crossed(2, 6, 3, 5)
    back(1, False)
    back(2, False)
    for j in range(2):
        recv(("cp", 4, j), Sb.at[zi(4), j])
        recv(("cm", 4, j + 2), Sb.at[zi(4), j + 2])
    across(4)
    crossed(4)
    back(0, False)
    Bk[...] = Ba[...].astype(BF16)
    recv("rs0", Rs.at[zl])
    recv("rs1", Rs.at[1 - zl])
    def partial(k, pair_of_parts, is_own):
        rows = [pl.ds(pl.multiple_of((k // 2) * 512 + h * 256 + pair_of_parts * 128, 128), 128) for h in range(2)]
        n = pl.ds((k % 2) * 4, 4)
        lhs = jnp.concatenate([Bk[i, :] for i in rows], axis=0)
        rhs = jnp.concatenate(
            [Rb[i, n, c].reshape(512, 128) for i in range(2)] + [Rs[i, n].reshape(512, 128) for i in range(2)],
            axis=1)
        res = lax.dot_general(lhs, rhs, (((1,), (1,)), ((), ())), preferred_element_type=F32)
        for i in range(2):
            u = 2 * pair_of_parts + i
            top, low = res[i * 64:i * 64 + 64], res[128 + i * 64:192 + i * 64]
            kept = top[:, 0:128]
            for j in range(4):
                at = slice(j * 128, (j + 1) * 128)
                Vb[k, j, 0, u] = top[:, at].astype(BF16)
                if j > 0:
                    kept = jnp.where(y == j, top[:, at], kept)
                if is_own:
                    W[1, u, j] = low[:, at]
                else:
                    Vb[k, j, 1, u] = low[:, at].astype(BF16)
            W[0, u, k] = kept

    def send_far(u):
        send(("dx", 1, u), Vb.at[s2, lo, 1, u], Ra.at[1, u, 0], xn(1))
        send(("dx", 3, u), Vb.at[s2, hi, 1, u], Ra.at[1, u, 1], xn(3))
        send(("dy", 1, u), Vb.at[lo, y2, 0, u], Ra.at[0, u, 0], yn(1))
        send(("dy", 3, u), Vb.at[hi, y2, 0, u], Ra.at[0, u, 1], yn(3))

    def send_near(u):
        for i, part, a, b, d in ((0, lo, sp, yp, 1), (1, hi, sm, ym, 3)):
            recv(("dx", d, u), Ra.at[1, u, i])
            Vb[a, part, 1, u] = (Vb[a, part, 1, u].astype(F32) + Ra[1, u, i].astype(F32)).astype(BF16)
            send(("nx", u), Vb.at[a, :, 1, u], Rd.at[1, u, i], xn(d))
            recv(("dy", d, u), Ra.at[0, u, i])
            Vb[part, b, 0, u] = (Vb[part, b, 0, u].astype(F32) + Ra[0, u, i].astype(F32)).astype(BF16)
            send(("ny", u), Vb.at[:, b, 0, u], Rd.at[0, u, i], yn(d))

    def send_small(u):
        for h, name, small, step in ((1, "nx", "ey", yn), (0, "ny", "ex", xn)):
            recv((name, u), Rd.at[h, u])
            total = W[h, u] + Rd[h, u, 0].astype(F32) + Rd[h, u, 1].astype(F32)
            W[h, u] = total
            Wb[h, u] = total.astype(BF16)
            for d in (2, 1, 3):
                at = (y + d) % 4 if h == 1 else (s0 + d) % 4
                send((small, u), Wb.at[h, u, at], X.at[h, u, d - 1], step(d))

    def send_final(u):
        for h, small, at in ((1, "ey", y), (0, "ex", s0)):
            recv((small, u), X.at[h, u])
            Fb[h, u] = W[h, u, at] + X[h, u, 0].astype(F32) + X[h, u, 1].astype(F32) + X[h, u, 2].astype(F32)
            send("f", Fb.at[h, u], upd.at[pl.ds(h * 256 + u * 64, 64)], final_to)

    begin()
    for i in range(2):
        for k in (s2, sp, sm):
            partial(k, i, False)
        partial(s0, i, True)
        send_far(2 * i)
        send_far(2 * i + 1)
    send_near(0)
    send_near(1)
    left_device(1)
    send_small(0)
    send_near(2)
    send_small(1)
    send_near(3)
    send_final(0)
    send_small(2)
    send_final(1)
    send_small(3)
    send_final(2)
    send_final(3)
    @pl.when(g_slot != 0)
    def _():
        for h in range(2):
            move(h).wait_send()

    left_device(2)
    recv("f", upd)
    for copy in outs:
        copy.wait()
    assert len(slots) <= SLOTS, len(slots)


def body(gradient, first_moment, second_moment, left_basis, right_basis):
    hbm = pl.BlockSpec(memory_space=pl.ANY)
    vm = pltpu.VMEM
    update, first_new, second_new = pl.pallas_call(
        kernel,
        out_shape=(
            jax.ShapeDtypeStruct((512, 128), F32),
            jax.ShapeDtypeStruct((512, 128), F32),
            jax.ShapeDtypeStruct((512, 128), F32),
        ),
        in_specs=[hbm] * 5,
        out_specs=(hbm, hbm, hbm),
        scratch_shapes=[
            vm((2, 256, 128), BF16),
            vm((4, 4, 2, 2, 256, 128), BF16),
            vm((4, 4, 2, 4, 2, 32, 256), BF16),
            vm((2, 8, 2, 128, 128), BF16),
            vm((2, 8, 128, 128), BF16),
            vm((256, 1024), BF16),
            vm((8, 2, 128, 256), F32),
            vm((8, 2, 128, 256), BF16),
            vm((4, 2, 128, 256), BF16),
            vm((4, 2, 128, 256), BF16),
            vm((8, 4, 128, 128), BF16),
            vm((8, 4, 128, 128), BF16),
            vm((1024, 512), F32),
            vm((1024, 512), BF16),
            vm((4, 4, 2, 4, 64, 128), BF16),
            vm((2, 4, 2, 2, 64, 128), BF16),
            vm((2, 4, 2, 4, 64, 128), BF16),
            vm((2, 4, 4, 64, 128), F32),
            vm((2, 4, 4, 64, 128), BF16),
            vm((2, 4, 3, 64, 128), BF16),
            vm((2, 4, 64, 128), F32),
            vm((512, 128), F32),
            vm((512, 128), F32),
            vm((512, 128), F32),
            vm((512, 128), F32),
            pltpu.SemaphoreType.DMA((8,)),
            pltpu.SemaphoreType.DMA((SLOTS,)),
            pltpu.SemaphoreType.DMA((5,)),
            pltpu.SemaphoreType.DMA((4,)),
        ],
        compiler_params=pltpu.CompilerParams(
            collective_id=0, has_side_effects=True, vmem_limit_bytes=63 * 2**20),
        cost_estimate=pl.CostEstimate(flops=5 * 10**9, bytes_accessed=10**7, transcendentals=10**5),
    )(
        gradient.reshape(2, 256, 128),
        left_basis,
        right_basis.reshape(8, 2, 128, 128),
        first_moment,
        second_moment,
    )
    return update, first_new, second_new


def solution(mesh):
    place = P("row", "col")
    placed = (place, place, place, P("col", "row"), place)
    return jax.shard_map(
        body, mesh=mesh, in_specs=placed, out_specs=(place, place, place), check_vma=False)
```

```python
import math

import jax
import jax.numpy as jnp
from jax import lax
from jax.experimental import pallas as pl
from jax.experimental.pallas import tpu as pltpu
from jax.sharding import PartitionSpec as P

STEP = 10
beta_one = 0.9
beta_two = 0.95
epsilon = 1e-08

MESH = pl.DeviceIdType.MESH
F32 = jnp.float32
BF16 = jnp.bfloat16
SLOTS = 160


def kernel(g, l, r, m, v, upd, fo, so, Gx, Gb, Lb, Rb, Rs, Tt, Qf, Qs, Bp, Bm, Sb, So, Ba, Bk,
           Vb, Ra, Rd, W, Wb, X, Fb, mb, vb, fb, sb, ssem, rsem, lsem, msem):
    zh = lax.axis_index("row")
    col = lax.axis_index("col")
    c = col % 2
    y = (col // 2) % 4
    zl = (col // 8) % 2
    x = col // 16
    z = 2 * zh + zl

    def dev(x_, y_, z_, c_):
        return (z_ // 2, ((x_ * 2 + z_ % 2) * 4 + y_) * 2 + c_)

    def xn(d):
        return dev((x + d) % 4, y, z, c)

    def yn(d):
        return dev(x, (y + d) % 4, z, c)

    def zn(d):
        return dev(x, y, (z + d) % 8, c)

    def half(k):
        return (1 + (k + 1) // 2) % 2

    sib = dev(x, y, z, 1 - c)
    pair = dev(x, y, 2 * zh + 1 - zl, c)
    b1, b0 = zh // 2, zh % 2
    g_slot = 2 * b0 + zl
    s0 = (x + 4 - zh) % 4
    mine = (zl + half(zh)) % 2
    final_to = dev(zh, y, 2 * (2 * mine + s0 // 2) + s0 % 2, c)
    final_from = dev((g_slot + x) % 4, y, 2 * x + (b1 + half(x)) % 2, c)
    xa = (x + 4 - g_slot) % 4
    z_to = 2 * xa + (b1 + half(xa)) % 2
    z_from = 2 * (2 * mine + s0 // 2) + s0 % 2
    l_slot = 2 * (x % 2) + zl
    t0 = (x + 2 - 2 * half(zh)) % 4
    l_to, l_from = [], []
    for d in range(4):
        k = (zh + d) % 4
        l_to.append(dev((l_slot + 2 - 2 * half(k)) % 4, y, 2 * k + (x // 2 + half(k)) % 2, c))
        k = (zh + 4 - d) % 4
        l_from.append(dev(2 * mine + t0 // 2, y, 2 * k + t0 % 2, c))

    slots = {}
    sent = []

    def slot(name):
        return slots.setdefault(name, len(slots))

    def begin():
        sent.append(0)

    def send(name, src, dst, to):
        k = slot(name)
        pltpu.make_async_remote_copy(
            src_ref=src, dst_ref=dst, send_sem=ssem.at[len(sent) - 1], recv_sem=rsem.at[k],
            device_id=to, device_id_type=MESH).start()
        sent[-1] += math.prod(dst.shape) * dst.dtype.itemsize

    def recv(name, dst):
        pltpu.make_async_remote_copy(
            src_ref=dst, dst_ref=dst, send_sem=ssem.at[0], recv_sem=rsem.at[slot(name)],
            device_id=sib, device_id_type=MESH).wait_recv()

    def left_device(phase):
        rest = sent[phase]
        for unit, ref in ((2**20, Gb), (2**18, Gb.at[0]), (2**17, Gb.at[0, 0]), (2**16, Gb.at[0, 0, 0]),
                          (2**12, Gb.at[0, 0, 0, 0])):
            n, rest = rest // unit, rest % unit
            while n > 0:
                now = min(n, ref.shape[0] if unit > 2**12 else 16)
                part = ref.at[pl.ds(0, now if unit > 2**12 else 16 * now)]
                pltpu.make_async_remote_copy(
                    src_ref=part, dst_ref=part, send_sem=ssem.at[phase], recv_sem=rsem.at[0],
                    device_id=sib, device_id_type=MESH).wait_send()
                n -= now
        assert rest == 0

    begin()
    own = [
        pltpu.make_async_copy(r, Rb.at[zl], lsem.at[0]),
        pltpu.make_async_copy(m, mb, lsem.at[1]),
        pltpu.make_async_copy(v, vb, lsem.at[2]),
    ]
    for copy in own:
        copy.start()

    barrier = pltpu.get_barrier_semaphore()
    partners = [final_to, final_from, sib, zn(1), zn(7)] + l_to + l_from
    partners += [dev(x, y, k, jnp.where(k == z, 1 - c, c)) for k in (z_to, z_from)]
    partners += [xn(d) for d in (1, 2, 3)] + [yn(d) for d in (1, 2, 3)]
    for p in partners:
        pl.semaphore_signal(barrier, inc=1, device_id=p, device_id_type=MESH)
    pl.semaphore_wait(barrier, len(partners))

    o = 1 - c
    lo, hi = pl.ds(0, 2), pl.ds(2, 2)
    full = slice(None)
    sm, sp, s2 = (s0 + 3) % 4, (s0 + 1) % 4, (s0 + 2) % 4
    tm, tp, t2 = (t0 + 3) % 4, (t0 + 1) % 4, (t0 + 2) % 4
    ym, yp, y2 = (y + 3) % 4, (y + 1) % 4, (y + 2) % 4

    def same(name, ref, to):
        send(name, ref, ref, to)

    def lplace(rel, low):
        return {2: 0, 0: 3}.get(rel, 1 + low if rel == 1 else 2 - low)

    for d in (2, 3, 1, 0):
        low = (x // 2 + half((zh + d) % 4)) % 2
        for h in range(2):
            send(("lp", d), l.at[:, pl.ds(h * 256, 256)], Lb.at[l_slot, y, c, lplace((4 - d) % 4, low), h], l_to[d])
    gm = [slot(("gm", h)) for h in range(2)]

    def move(h):
        return pltpu.make_async_remote_copy(
            src_ref=g.at[h], dst_ref=Gx.at[h], send_sem=msem.at[h], recv_sem=rsem.at[gm[h]],
            device_id=dev((x + g_slot) % 4, y, z, c), device_id_type=MESH)

    @pl.when(g_slot != 0)
    def _():
        for h in range(2):
            move(h).start()

    @pl.when(g_slot == 0)
    def _():
        for h in range(2):
            pltpu.make_async_copy(g.at[h], Gx.at[h], rsem.at[gm[h]]).start()

    send("rs0", r.at[:, o], Rs.at[zl], sib)
    gp = [slot(("gp", h)) for h in range(2)]

    def rise(h):
        return pltpu.make_async_remote_copy(
            src_ref=Gx.at[h], dst_ref=Gb.at[g_slot, y, c, h], send_sem=msem.at[2 + h], recv_sem=rsem.at[gp[h]],
            device_id=dev(x, y, z_to, c), device_id_type=MESH)

    for h in range(2):
        @pl.when(g_slot != 0)
        def _():
            move(h).wait_recv()

        @pl.when(g_slot == 0)
        def _():
            pltpu.make_async_copy(g.at[h], Gx.at[h], rsem.at[gm[h]]).wait()

        @pl.when(z_to != z)
        def _():
            rise(h).start()

        @pl.when(z_to == z)
        def _():
            pltpu.make_async_copy(Gx.at[h], Gb.at[g_slot, y, c, h], rsem.at[gp[h]]).start()

    def gperm(h):
        @pl.when(z_from != z)
        def _():
            pltpu.make_async_remote_copy(
                src_ref=Gx.at[h], dst_ref=Gb.at[s0, y, c, h], send_sem=msem.at[2 + h], recv_sem=rsem.at[gp[h]],
                device_id=sib, device_id_type=MESH).wait_recv()

        @pl.when(z_from == z)
        def _():
            pltpu.make_async_copy(Gx.at[h], Gb.at[s0, y, c, h], rsem.at[gp[h]]).wait()

    lcols = (pl.ds(0, 1), pl.ds(1, 2), pl.ds(3, 1))

    def lp_(j, h, a, b):
        return Lb.at[a, b, c, lcols[j], h]

    for d in (2, 3, 1, 0):
        recv(("lp", d), Lb.at[t0, y, c, lplace((4 - d) % 4, zl)])
    for d in (2, 1, 3):
        same("lx", Lb.at[t0, y, c, :, 0], xn(d))
        same("ly", Lb.at[t0, y, c, :, 1], yn(d))

    def lbig(j):
        for d in (1, 3):
            same(("Ly", d, j), lp_(j, 0, full, y), yn(d))
            same(("Lx", d, j), lp_(j, 1, t0, full), xn(d))

    def lfwd(j):
        recv(("Ly", 1, j), lp_(j, 0, full, ym))
        same(("Lyf", j), lp_(j, 0, lo, ym), yn(1))
        recv(("Ly", 3, j), lp_(j, 0, full, yp))
        same(("Lyf", j), lp_(j, 0, hi, yp), yn(3))
        recv(("Lx", 1, j), lp_(j, 1, tm, full))
        same(("Lxf", j), lp_(j, 1, tm, lo), xn(1))
        recv(("Lx", 3, j), lp_(j, 1, tp, full))
        same(("Lxf", j), lp_(j, 1, tp, hi), xn(3))

    def lshare(j):
        recv(("Lyf", j), lp_(j, 0, full, y2))
        recv(("Lxf", j), lp_(j, 1, t2, full))
        for i in {0: (0,), 1: (1, 2), 2: (3,)}[j]:
            same(("Ls", i), Lb.at[:, :, c, i], sib)

    def lwait(i):
        recv(("Ls", i), Lb.at[:, :, o, i])

    @pl.when(z_to != z)
    def _():
        for h in range(2):
            rise(h).wait_send()

    send("rp", r, Rb.at[zl], pair)
    three = pl.ds(0, 3)
    gperm(0)
    for d in (2, 1, 3):
        same("gx", Gb.at[s0, y, c, 0], xn(d))
    gperm(1)
    for d in (2, 1, 3):
        same("gy", Gb.at[s0, y, c, 1], yn(d))
    recv("lx", Lb.at[three, y, c, :, 0])
    recv("ly", Lb.at[t0, three, c, :, 1])
    lbig(0)

    recv("gx", Gb.at[three, y, c, 0])
    same("Gy1a", Gb.at[lo, y, c, 0], yn(1))
    same("Gy3b", Gb.at[hi, y, c, 0], yn(3))
    same("Gy1b", Gb.at[hi, y, c, 0], yn(1))
    same("Gy3a", Gb.at[lo, y, c, 0], yn(3))
    recv("gy", Gb.at[s0, three, c, 1])
    same("Gx1a", Gb.at[s0, lo, c, 1], xn(1))
    same("Gx3b", Gb.at[s0, hi, c, 1], xn(3))
    same("Gx1b", Gb.at[s0, hi, c, 1], xn(1))
    same("Gx3a", Gb.at[s0, lo, c, 1], xn(3))
    same("Gs0", Gb.at[:, y, c, 0], sib)
    same("Gs1", Gb.at[s0, :, c, 1], sib)
    lfwd(0)
    recv("Gy1a", Gb.at[lo, ym, c, 0])
    same("Gyf", Gb.at[lo, ym, c, 0], yn(1))
    recv("Gy3b", Gb.at[hi, yp, c, 0])
    same("Gyf", Gb.at[hi, yp, c, 0], yn(3))
    recv("Gx1a", Gb.at[sm, lo, c, 1])
    same("Gxf", Gb.at[sm, lo, c, 1], xn(1))
    recv("Gx3b", Gb.at[sp, hi, c, 1])
    same("Gxf", Gb.at[sp, hi, c, 1], xn(3))
    lbig(1)
    recv("Gy1b", Gb.at[hi, ym, c, 0])
    same("Gs0", Gb.at[:, ym, c, 0], sib)
    recv("Gy3a", Gb.at[lo, yp, c, 0])
    same("Gs0", Gb.at[:, yp, c, 0], sib)
    recv("Gx1b", Gb.at[sm, hi, c, 1])
    same("Gs1", Gb.at[sm, :, c, 1], sib)
    recv("Gx3a", Gb.at[sp, lo, c, 1])
    same("Gs1", Gb.at[sp, :, c, 1], sib)
    recv("Gyf", Gb.at[:, y2, c, 0])
    same("Gs0", Gb.at[:, y2, c, 0], sib)
    recv("Gxf", Gb.at[s2, :, c, 1])
    same("Gs1", Gb.at[s2, :, c, 1], sib)
    lshare(0)
    recv("rp", Rb.at[1 - zl])
    send("rs1", Rb.at[1 - zl, :, o], Rs.at[1 - zl], sib)

    own[0].wait()
    def turn(b, h):
        lhs = jnp.concatenate(
            [Gb[2 * b + i, j, k, h] for i in range(2) for j in range(4) for k in range(2)], axis=1)
        rhs = jnp.concatenate([Rb[i].reshape(2048, 128) for i in range(2)], axis=1)
        t = jnp.dot(lhs, rhs, preferred_element_type=F32)
        q = 2 * b + h
        Tt[:, q * 256:(q + 1) * 256] = t.T.astype(BF16)

    recv("Gs0", Gb.at[:, :, o, 0])
    turn(0, 0)
    turn(1, 0)
    lfwd(1)
    recv("Gs1", Gb.at[:, :, o, 1])
    turn(0, 1)
    turn(1, 1)

    lwait(0)

    def left(j):
        return jnp.concatenate([Lb[:, :, :, j, h].reshape(1024, 256) for h in range(2)], axis=1)

    rels = (2, 1 + 2 * zl, 3 - 2 * zl, 0)

    def rotate(p):
        k = (zh + rels[p]) % 4
        q = jnp.dot(Tt[...], left(p), preferred_element_type=F32)
        for i in range(2):
            for j in range(4):
                part = q[i * 128:(i + 1) * 128, j * 128:(j + 1) * 128]
                Qf[2 * k + i, j] = part
                Qs[2 * k + i, j] = part.astype(BF16)

    def zi(d):
        return (z + d) % 8

    ha, hb = pl.ds(0, 64), pl.ds(64, 64)
    rotate(0)
    for j in range(4):
        send(("bp", 1, j), Qs.at[zi(4), j, ha], Bp.at[0, j, ha], zn(1))
        send(("bm", 1, j), Qs.at[zi(4), j, hb], Bm.at[0, j, hb], zn(7))
    lshare(1)
    lbig(2)
    lwait(1)
    rotate(1)
    send("bpe", Qs.at[zi(3), :, hb], Bp.at[1, :, hb], zn(1))
    send("bme", Qs.at[zi(5), :, ha], Bm.at[1, :, ha], zn(7))

    for j in range(4):
        k = zi(3)
        recv(("bp", 1, j), Bp.at[0, j, ha])
        Qs[k, j, ha] = (Qf[k, j, ha] + Bp[0, j, ha].astype(F32)).astype(BF16)
        send(("bp", 2, j), Qs.at[k, j, ha], Bp.at[1, j, ha], zn(1))
        k = zi(5)
        recv(("bm", 1, j), Bm.at[0, j, hb])
        Qs[k, j, hb] = (Qf[k, j, hb] + Bm[0, j, hb].astype(F32)).astype(BF16)
        send(("bm", 2, j), Qs.at[k, j, hb], Bm.at[1, j, hb], zn(7))
    lwait(2)
    rotate(2)
    lfwd(2)
    recv("bpe", Bp.at[1, :, hb])
    recv("bme", Bm.at[1, :, ha])
    for s in (3, 4):
        for j in range(4):
            k = zi(5 - s)
            recv(("bp", s - 1, j), Bp.at[s - 2, j] if s > 3 else Bp.at[1, j, ha])
            Qs[k, j] = (Qf[k, j] + Bp[s - 2, j].astype(F32)).astype(BF16)
            send(("bp", s, j), Qs.at[k, j], Bp.at[s - 1, j], zn(1))
            k = zi(3 + s)
            recv(("bm", s - 1, j), Bm.at[s - 2, j] if s > 3 else Bm.at[1, j, hb])
            Qs[k, j] = (Qf[k, j] + Bm[s - 2, j].astype(F32)).astype(BF16)
            send(("bm", s, j), Qs.at[k, j], Bm.at[s - 1, j], zn(7))
        if s == 3:
            lshare(2)
            lwait(3)
            rotate(3)
    own[1].wait()
    own[2].wait()
    begin()
    for j in range(4):
        recv(("bp", 4, j), Bp.at[3, j])
        recv(("bm", 4, j), Bm.at[3, j])
        rows = slice(j * 128, (j + 1) * 128)
        rotated = (Qf[z, j] + Bp[3, j].astype(F32) + Bm[3, j].astype(F32)).T
        first = beta_one * mb[rows] + (1.0 - beta_one) * rotated
        second = beta_two * vb[rows] + (1.0 - beta_two) * rotated * rotated
        one = first * (1.0 / (1.0 - beta_one**STEP))
        two = second * (1.0 / (1.0 - beta_two**STEP))
        Sb[z, j] = (one / (jnp.sqrt(two) + epsilon)).astype(BF16)
        same(("cp", 1, j), Sb.at[z, j], zn(1))
        same(("cm", 1, j), Sb.at[z, j], zn(7))
        fb[rows] = first
        sb[rows] = second
    outs = [pltpu.make_async_copy(fb, fo, lsem.at[3]), pltpu.make_async_copy(sb, so, lsem.at[4])]
    for copy in outs:
        copy.start()

    left_device(0)
    def across(d):
        send(("ss", d), Sb.at[zi(d)], So.at[zi(d)], sib)

    def crossed(*ds):
        for d in ds:
            recv(("ss", d), So.at[zi(d)])

    def back(j):
        k = (zh + rels[j]) % 4
        s = jnp.concatenate(
            [ref[2 * k + i].reshape(512, 128) for ref in (Sb, So) for i in range(2)], axis=1)
        part = jnp.dot(left(j), s, preferred_element_type=F32)
        if j == 3:
            Ba[...] = part
        elif j > 0:
            Ba[...] += part
        else:
            Bk[...] = (Ba[...] + part).astype(BF16)

    across(0)
    for s in (2, 3):
        for j in range(4):
            recv(("cp", s - 1, j), Sb.at[zi(9 - s), j])
            same(("cp", s, j), Sb.at[zi(9 - s), j], zn(1))
            recv(("cm", s - 1, j), Sb.at[zi(s - 1), j])
            same(("cm", s, j), Sb.at[zi(s - 1), j], zn(7))
        across(9 - s)
        across(s - 1)
    crossed(0, 1, 7)
    back(3)
    for j in range(2):
        recv(("cp", 3, j), Sb.at[zi(5), j])
        same(("cp", 4, j), Sb.at[zi(5), j], zn(1))
        recv(("cm", 3, j + 2), Sb.at[zi(3), j + 2])
        same(("cm", 4, j + 2), Sb.at[zi(3), j + 2], zn(7))
    crossed(2, 6)
    back(2)
    for j in range(2):
        recv(("cp", 3, j + 2), Sb.at[zi(5), j + 2])
        recv(("cm", 3, j), Sb.at[zi(3), j])
    across(5)
    across(3)
    crossed(3, 5)
    back(1)
    for j in range(2):
        recv(("cp", 4, j), Sb.at[zi(4), j])
        recv(("cm", 4, j + 2), Sb.at[zi(4), j + 2])
    across(4)
    crossed(4)
    back(0)
    recv("rs0", Rs.at[zl])
    recv("rs1", Rs.at[1 - zl])
    def partial(k, pair_of_parts, is_own):
        rows = [pl.ds(pl.multiple_of((k // 2) * 512 + h * 256 + pair_of_parts * 128, 128), 128) for h in range(2)]
        n = pl.ds((k % 2) * 4, 4)
        lhs = jnp.concatenate([Bk[i, :] for i in rows], axis=0)
        rhs = jnp.concatenate(
            [Rb[i, n, c].reshape(512, 128) for i in range(2)] + [Rs[i, n].reshape(512, 128) for i in range(2)],
            axis=1)
        res = lax.dot_general(lhs, rhs, (((1,), (1,)), ((), ())), preferred_element_type=F32)
        for i in range(2):
            u = 2 * pair_of_parts + i
            top, low = res[i * 64:i * 64 + 64], res[128 + i * 64:192 + i * 64]
            kept = top[:, 0:128]
            for j in range(4):
                at = slice(j * 128, (j + 1) * 128)
                Vb[k, j, 0, u] = top[:, at].astype(BF16)
                if j > 0:
                    kept = jnp.where(y == j, top[:, at], kept)
                if is_own:
                    W[1, u, j] = low[:, at]
                else:
                    Vb[k, j, 1, u] = low[:, at].astype(BF16)
            W[0, u, k] = kept

    def send_far(u):
        send(("dx", 1, u), Vb.at[s2, lo, 1, u], Ra.at[1, u, 0], xn(1))
        send(("dx", 3, u), Vb.at[s2, hi, 1, u], Ra.at[1, u, 1], xn(3))
        send(("dy", 1, u), Vb.at[lo, y2, 0, u], Ra.at[0, u, 0], yn(1))
        send(("dy", 3, u), Vb.at[hi, y2, 0, u], Ra.at[0, u, 1], yn(3))

    def send_near(u):
        for i, part, a, b, d in ((0, lo, sp, yp, 1), (1, hi, sm, ym, 3)):
            recv(("dx", d, u), Ra.at[1, u, i])
            Vb[a, part, 1, u] = (Vb[a, part, 1, u].astype(F32) + Ra[1, u, i].astype(F32)).astype(BF16)
            send(("nx", u), Vb.at[a, :, 1, u], Rd.at[1, u, i], xn(d))
            recv(("dy", d, u), Ra.at[0, u, i])
            Vb[part, b, 0, u] = (Vb[part, b, 0, u].astype(F32) + Ra[0, u, i].astype(F32)).astype(BF16)
            send(("ny", u), Vb.at[:, b, 0, u], Rd.at[0, u, i], yn(d))

    def send_small(u):
        for h, name, small, step in ((1, "nx", "ey", yn), (0, "ny", "ex", xn)):
            recv((name, u), Rd.at[h, u])
            total = W[h, u] + Rd[h, u, 0].astype(F32) + Rd[h, u, 1].astype(F32)
            W[h, u] = total
            Wb[h, u] = total.astype(BF16)
            for d in (2, 1, 3):
                at = (y + d) % 4 if h == 1 else (s0 + d) % 4
                send((small, u), Wb.at[h, u, at], X.at[h, u, d - 1], step(d))

    def send_final(u):
        for h, small, at in ((1, "ey", y), (0, "ex", s0)):
            recv((small, u), X.at[h, u])
            Fb[h, u] = W[h, u, at] + X[h, u, 0].astype(F32) + X[h, u, 1].astype(F32) + X[h, u, 2].astype(F32)
            send("f", Fb.at[h, u], upd.at[pl.ds(h * 256 + u * 64, 64)], final_to)

    begin()
    for i in range(2):
        for k in (s2, sp, sm):
            partial(k, i, False)
        partial(s0, i, True)
        send_far(2 * i)
        send_far(2 * i + 1)
    send_near(0)
    send_near(1)
    left_device(1)
    send_small(0)
    send_near(2)
    send_small(1)
    send_near(3)
    send_final(0)
    send_small(2)
    send_final(1)
    send_small(3)
    send_final(2)
    send_final(3)
    @pl.when(g_slot != 0)
    def _():
        for h in range(2):
            move(h).wait_send()

    left_device(2)
    recv("f", upd)
    for copy in outs:
        copy.wait()
    assert len(slots) <= SLOTS, len(slots)


def hand_over(a, b, c, a_out, b_out, c_out, buf, sem):
    there = [pltpu.make_async_copy(src, buf.at[i], sem.at[i]) for i, src in enumerate((a, b, c))]
    back = [pltpu.make_async_copy(buf.at[i], dst, sem.at[3 + i]) for i, dst in enumerate((a_out, b_out, c_out))]
    for copy in there:
        copy.start()
    for i in range(3):
        there[i].wait()
        back[i].start()
    for copy in back:
        copy.wait()


def body(gradient, first_moment, second_moment, left_basis, right_basis):
    hbm = pl.BlockSpec(memory_space=pl.ANY)
    vm = pltpu.VMEM
    update, first_new, second_new = pl.pallas_call(
        kernel,
        out_shape=(
            jax.ShapeDtypeStruct((512, 128), F32),
            jax.ShapeDtypeStruct((512, 128), F32),
            jax.ShapeDtypeStruct((512, 128), F32),
        ),
        in_specs=[hbm] * 5,
        out_specs=(hbm, hbm, hbm),
        scratch_shapes=[
            vm((2, 256, 128), BF16),
            vm((4, 4, 2, 2, 256, 128), BF16),
            vm((4, 4, 2, 4, 2, 32, 256), BF16),
            vm((2, 8, 2, 128, 128), BF16),
            vm((2, 8, 128, 128), BF16),
            vm((256, 1024), BF16),
            vm((8, 4, 128, 128), F32),
            vm((8, 4, 128, 128), BF16),
            vm((4, 4, 128, 128), BF16),
            vm((4, 4, 128, 128), BF16),
            vm((8, 4, 128, 128), BF16),
            vm((8, 4, 128, 128), BF16),
            vm((1024, 512), F32),
            vm((1024, 512), BF16),
            vm((4, 4, 2, 4, 64, 128), BF16),
            vm((2, 4, 2, 2, 64, 128), BF16),
            vm((2, 4, 2, 4, 64, 128), BF16),
            vm((2, 4, 4, 64, 128), F32),
            vm((2, 4, 4, 64, 128), BF16),
            vm((2, 4, 3, 64, 128), BF16),
            vm((2, 4, 64, 128), F32),
            vm((512, 128), F32),
            vm((512, 128), F32),
            vm((512, 128), F32),
            vm((512, 128), F32),
            pltpu.SemaphoreType.DMA((8,)),
            pltpu.SemaphoreType.DMA((SLOTS,)),
            pltpu.SemaphoreType.DMA((5,)),
            pltpu.SemaphoreType.DMA((4,)),
        ],
        compiler_params=pltpu.CompilerParams(
            collective_id=0, has_side_effects=True, vmem_limit_bytes=63 * 2**20),
        cost_estimate=pl.CostEstimate(flops=5 * 10**9, bytes_accessed=10**7, transcendentals=10**5),
    )(
        gradient.reshape(2, 256, 128),
        left_basis,
        right_basis.reshape(8, 2, 128, 128),
        first_moment,
        second_moment,
    )
    whole = jax.ShapeDtypeStruct((512, 128), F32)
    return pl.pallas_call(
        hand_over,
        out_shape=(whole, whole, whole),
        in_specs=[hbm] * 3,
        out_specs=(hbm, hbm, hbm),
        scratch_shapes=[vm((3, 512, 128), F32), pltpu.SemaphoreType.DMA((6,))],
        compiler_params=pltpu.CompilerParams(vmem_limit_bytes=63 * 2**20),
    )(update, first_new, second_new)


def solution(mesh):
    place = P("row", "col")
    placed = (place, place, place, P("col", "row"), place)
    return jax.shard_map(
        body, mesh=mesh, in_specs=placed, out_specs=(place, place, place), check_vma=False)
```

```python
import math

import jax
import jax.numpy as jnp
from jax import lax
from jax.experimental import pallas as pl
from jax.experimental.pallas import tpu as pltpu
from jax.sharding import PartitionSpec as P

STEP = 10
beta_one = 0.9
beta_two = 0.95
epsilon = 1e-08

MESH = pl.DeviceIdType.MESH
F32 = jnp.float32
BF16 = jnp.bfloat16
SLOTS = 160


def kernel(g, l, r, m, v, upd, fo, so, Gx, Gb, Lb, Rb, Rs, Tt, Qf, Qs, Bp, Bm, Sb, So, Ba, Bk,
           Vb, Ra, Rd, W, Wb, X, Fb, mb, vb, fb, sb, ssem, rsem, lsem, msem):
    zh = lax.axis_index("row")
    col = lax.axis_index("col")
    c = col % 2
    y = (col // 2) % 4
    zl = (col // 8) % 2
    x = col // 16
    z = 2 * zh + zl

    def dev(x_, y_, z_, c_):
        return (z_ // 2, ((x_ * 2 + z_ % 2) * 4 + y_) * 2 + c_)

    def xn(d):
        return dev((x + d) % 4, y, z, c)

    def yn(d):
        return dev(x, (y + d) % 4, z, c)

    def zn(d):
        return dev(x, y, (z + d) % 8, c)

    def half(k):
        return (1 + (k + 1) // 2) % 2

    sib = dev(x, y, z, 1 - c)
    pair = dev(x, y, 2 * zh + 1 - zl, c)
    b1, b0 = zh // 2, zh % 2
    g_slot = 2 * b0 + zl
    s0 = (x + 4 - zh) % 4
    mine = (zl + half(zh)) % 2
    final_to = dev(zh, y, 2 * (2 * mine + s0 // 2) + s0 % 2, c)
    final_from = dev((g_slot + x) % 4, y, 2 * x + (b1 + half(x)) % 2, c)
    xa = (x + 4 - g_slot) % 4
    z_to = 2 * xa + (b1 + half(xa)) % 2
    z_from = 2 * (2 * mine + s0 // 2) + s0 % 2
    l_slot = 2 * (x % 2) + zl
    t0 = (x + 2 - 2 * half(zh)) % 4
    l_to, l_from = [], []
    for d in range(4):
        k = (zh + d) % 4
        l_to.append(dev((l_slot + 2 - 2 * half(k)) % 4, y, 2 * k + (x // 2 + half(k)) % 2, c))
        k = (zh + 4 - d) % 4
        l_from.append(dev(2 * mine + t0 // 2, y, 2 * k + t0 % 2, c))

    slots = {}
    sent = []

    def slot(name):
        return slots.setdefault(name, len(slots))

    def begin():
        sent.append(0)

    def send(name, src, dst, to):
        k = slot(name)
        pltpu.make_async_remote_copy(
            src_ref=src, dst_ref=dst, send_sem=ssem.at[len(sent) - 1], recv_sem=rsem.at[k],
            device_id=to, device_id_type=MESH).start()
        sent[-1] += math.prod(dst.shape) * dst.dtype.itemsize

    def recv(name, dst):
        pltpu.make_async_remote_copy(
            src_ref=dst, dst_ref=dst, send_sem=ssem.at[0], recv_sem=rsem.at[slot(name)],
            device_id=sib, device_id_type=MESH).wait_recv()

    def left_device(phase):
        rest = sent[phase]
        for unit, ref in ((2**20, Gb), (2**18, Gb.at[0]), (2**17, Gb.at[0, 0]), (2**16, Gb.at[0, 0, 0]),
                          (2**12, Gb.at[0, 0, 0, 0])):
            n, rest = rest // unit, rest % unit
            while n > 0:
                now = min(n, ref.shape[0] if unit > 2**12 else 16)
                part = ref.at[pl.ds(0, now if unit > 2**12 else 16 * now)]
                pltpu.make_async_remote_copy(
                    src_ref=part, dst_ref=part, send_sem=ssem.at[phase], recv_sem=rsem.at[0],
                    device_id=sib, device_id_type=MESH).wait_send()
                n -= now
        assert rest == 0

    begin()
    own = [
        pltpu.make_async_copy(r, Rb.at[zl], lsem.at[0]),
        pltpu.make_async_copy(m, mb, lsem.at[1]),
        pltpu.make_async_copy(v, vb, lsem.at[2]),
    ]
    for copy in own:
        copy.start()

    barrier = pltpu.get_barrier_semaphore()
    partners = [final_to, final_from, sib, zn(1), zn(7)] + l_to + l_from
    partners += [dev(x, y, k, jnp.where(k == z, 1 - c, c)) for k in (z_to, z_from)]
    partners += [xn(d) for d in (1, 2, 3)] + [yn(d) for d in (1, 2, 3)]
    for p in partners:
        pl.semaphore_signal(barrier, inc=1, device_id=p, device_id_type=MESH)
    pl.semaphore_wait(barrier, len(partners))

    o = 1 - c
    lo, hi = pl.ds(0, 2), pl.ds(2, 2)
    full = slice(None)
    sm, sp, s2 = (s0 + 3) % 4, (s0 + 1) % 4, (s0 + 2) % 4
    tm, tp, t2 = (t0 + 3) % 4, (t0 + 1) % 4, (t0 + 2) % 4
    ym, yp, y2 = (y + 3) % 4, (y + 1) % 4, (y + 2) % 4

    def same(name, ref, to):
        send(name, ref, ref, to)

    def lplace(rel, low):
        return {2: 0, 0: 3}.get(rel, 1 + low if rel == 1 else 2 - low)

    for d in (2, 3, 1, 0):
        low = (x // 2 + half((zh + d) % 4)) % 2
        for h in range(2):
            send(("lp", d), l.at[:, pl.ds(h * 256, 256)], Lb.at[l_slot, y, c, lplace((4 - d) % 4, low), h], l_to[d])
    gm = [slot(("gm", h)) for h in range(2)]

    def move(h):
        return pltpu.make_async_remote_copy(
            src_ref=g.at[h], dst_ref=Gx.at[h], send_sem=msem.at[h], recv_sem=rsem.at[gm[h]],
            device_id=dev((x + g_slot) % 4, y, z, c), device_id_type=MESH)

    @pl.when(g_slot != 0)
    def _():
        for h in range(2):
            move(h).start()

    @pl.when(g_slot == 0)
    def _():
        for h in range(2):
            pltpu.make_async_copy(g.at[h], Gx.at[h], rsem.at[gm[h]]).start()

    send("rs0", r.at[:, o], Rs.at[zl], sib)
    gp = [slot(("gp", h)) for h in range(2)]

    def rise(h):
        return pltpu.make_async_remote_copy(
            src_ref=Gx.at[h], dst_ref=Gb.at[g_slot, y, c, h], send_sem=msem.at[2 + h], recv_sem=rsem.at[gp[h]],
            device_id=dev(x, y, z_to, c), device_id_type=MESH)

    for h in range(2):
        @pl.when(g_slot != 0)
        def _():
            move(h).wait_recv()

        @pl.when(g_slot == 0)
        def _():
            pltpu.make_async_copy(g.at[h], Gx.at[h], rsem.at[gm[h]]).wait()

        @pl.when(z_to != z)
        def _():
            rise(h).start()

        @pl.when(z_to == z)
        def _():
            pltpu.make_async_copy(Gx.at[h], Gb.at[g_slot, y, c, h], rsem.at[gp[h]]).start()

    def gperm(h):
        @pl.when(z_from != z)
        def _():
            pltpu.make_async_remote_copy(
                src_ref=Gx.at[h], dst_ref=Gb.at[s0, y, c, h], send_sem=msem.at[2 + h], recv_sem=rsem.at[gp[h]],
                device_id=sib, device_id_type=MESH).wait_recv()

        @pl.when(z_from == z)
        def _():
            pltpu.make_async_copy(Gx.at[h], Gb.at[s0, y, c, h], rsem.at[gp[h]]).wait()

    lcols = (pl.ds(0, 1), pl.ds(1, 2), pl.ds(3, 1))

    def lp_(j, h, a, b):
        return Lb.at[a, b, c, lcols[j], h]

    for d in (2, 3, 1, 0):
        recv(("lp", d), Lb.at[t0, y, c, lplace((4 - d) % 4, zl)])
    for d in (2, 1, 3):
        same("lx", Lb.at[t0, y, c, :, 0], xn(d))
        same("ly", Lb.at[t0, y, c, :, 1], yn(d))

    def lbig(j):
        for d in (1, 3):
            same(("Ly", d, j), lp_(j, 0, full, y), yn(d))
            same(("Lx", d, j), lp_(j, 1, t0, full), xn(d))

    def lfwd(j):
        recv(("Ly", 1, j), lp_(j, 0, full, ym))
        same(("Lyf", j), lp_(j, 0, lo, ym), yn(1))
        recv(("Ly", 3, j), lp_(j, 0, full, yp))
        same(("Lyf", j), lp_(j, 0, hi, yp), yn(3))
        recv(("Lx", 1, j), lp_(j, 1, tm, full))
        same(("Lxf", j), lp_(j, 1, tm, lo), xn(1))
        recv(("Lx", 3, j), lp_(j, 1, tp, full))
        same(("Lxf", j), lp_(j, 1, tp, hi), xn(3))

    def lshare(j):
        recv(("Lyf", j), lp_(j, 0, full, y2))
        recv(("Lxf", j), lp_(j, 1, t2, full))
        for i in {0: (0,), 1: (1, 2), 2: (3,)}[j]:
            same(("Ls", i), Lb.at[:, :, c, i], sib)

    def lwait(i):
        recv(("Ls", i), Lb.at[:, :, o, i])

    @pl.when(z_to != z)
    def _():
        for h in range(2):
            rise(h).wait_send()

    send("rp", r, Rb.at[zl], pair)
    three = pl.ds(0, 3)
    gperm(0)
    for d in (2, 1, 3):
        same("gx", Gb.at[s0, y, c, 0], xn(d))
    gperm(1)
    for d in (2, 1, 3):
        same("gy", Gb.at[s0, y, c, 1], yn(d))
    recv("lx", Lb.at[three, y, c, :, 0])
    recv("ly", Lb.at[t0, three, c, :, 1])
    lbig(0)

    recv("gx", Gb.at[three, y, c, 0])
    same("Gy1a", Gb.at[lo, y, c, 0], yn(1))
    same("Gy3b", Gb.at[hi, y, c, 0], yn(3))
    same("Gy1b", Gb.at[hi, y, c, 0], yn(1))
    same("Gy3a", Gb.at[lo, y, c, 0], yn(3))
    recv("gy", Gb.at[s0, three, c, 1])
    same("Gx1a", Gb.at[s0, lo, c, 1], xn(1))
    same("Gx3b", Gb.at[s0, hi, c, 1], xn(3))
    same("Gx1b", Gb.at[s0, hi, c, 1], xn(1))
    same("Gx3a", Gb.at[s0, lo, c, 1], xn(3))
    same("Gs0", Gb.at[:, y, c, 0], sib)
    same("Gs1", Gb.at[s0, :, c, 1], sib)
    lfwd(0)
    recv("Gy1a", Gb.at[lo, ym, c, 0])
    same("Gyf", Gb.at[lo, ym, c, 0], yn(1))
    recv("Gy3b", Gb.at[hi, yp, c, 0])
    same("Gyf", Gb.at[hi, yp, c, 0], yn(3))
    recv("Gx1a", Gb.at[sm, lo, c, 1])
    same("Gxf", Gb.at[sm, lo, c, 1], xn(1))
    recv("Gx3b", Gb.at[sp, hi, c, 1])
    same("Gxf", Gb.at[sp, hi, c, 1], xn(3))
    lbig(1)
    recv("Gy1b", Gb.at[hi, ym, c, 0])
    same("Gs0", Gb.at[:, ym, c, 0], sib)
    recv("Gy3a", Gb.at[lo, yp, c, 0])
    same("Gs0", Gb.at[:, yp, c, 0], sib)
    recv("Gx1b", Gb.at[sm, hi, c, 1])
    same("Gs1", Gb.at[sm, :, c, 1], sib)
    recv("Gx3a", Gb.at[sp, lo, c, 1])
    same("Gs1", Gb.at[sp, :, c, 1], sib)
    recv("Gyf", Gb.at[:, y2, c, 0])
    same("Gs0", Gb.at[:, y2, c, 0], sib)
    recv("Gxf", Gb.at[s2, :, c, 1])
    same("Gs1", Gb.at[s2, :, c, 1], sib)
    lshare(0)
    recv("rp", Rb.at[1 - zl])
    send("rs1", Rb.at[1 - zl, :, o], Rs.at[1 - zl], sib)

    own[0].wait()
    def turn(b, h):
        lhs = jnp.concatenate(
            [Gb[2 * b + i, j, k, h] for i in range(2) for j in range(4) for k in range(2)], axis=1)
        rhs = jnp.concatenate([Rb[i].reshape(2048, 128) for i in range(2)], axis=1)
        t = jnp.dot(lhs, rhs, preferred_element_type=F32)
        q = 2 * b + h
        Tt[:, q * 256:(q + 1) * 256] = t.T.astype(BF16)

    recv("Gs0", Gb.at[:, :, o, 0])
    turn(0, 0)
    turn(1, 0)
    lfwd(1)
    recv("Gs1", Gb.at[:, :, o, 1])
    turn(0, 1)
    turn(1, 1)

    lwait(0)

    def left(j):
        return jnp.concatenate([Lb[:, :, :, j, h].reshape(1024, 256) for h in range(2)], axis=1)

    rels = (2, 1 + 2 * zl, 3 - 2 * zl, 0)

    def rotate(p):
        k = (zh + rels[p]) % 4
        q = jnp.dot(Tt[...], left(p), preferred_element_type=F32)
        for i in range(2):
            for j in range(4):
                part = q[i * 128:(i + 1) * 128, j * 128:(j + 1) * 128]
                Qf[2 * k + i, j] = part
                Qs[2 * k + i, j] = part.astype(BF16)

    def zi(d):
        return (z + d) % 8

    ha, hb = pl.ds(0, 64), pl.ds(64, 64)
    rotate(0)
    for j in range(4):
        send(("bp", 1, j), Qs.at[zi(4), j, ha], Bp.at[0, j, ha], zn(1))
        send(("bm", 1, j), Qs.at[zi(4), j, hb], Bm.at[0, j, hb], zn(7))
    lshare(1)
    lbig(2)
    lwait(1)
    rotate(1)
    send("bpe", Qs.at[zi(3), :, hb], Bp.at[1, :, hb], zn(1))
    send("bme", Qs.at[zi(5), :, ha], Bm.at[1, :, ha], zn(7))

    for j in range(4):
        k = zi(3)
        recv(("bp", 1, j), Bp.at[0, j, ha])
        Qs[k, j, ha] = (Qf[k, j, ha] + Bp[0, j, ha].astype(F32)).astype(BF16)
        send(("bp", 2, j), Qs.at[k, j, ha], Bp.at[1, j, ha], zn(1))
        k = zi(5)
        recv(("bm", 1, j), Bm.at[0, j, hb])
        Qs[k, j, hb] = (Qf[k, j, hb] + Bm[0, j, hb].astype(F32)).astype(BF16)
        send(("bm", 2, j), Qs.at[k, j, hb], Bm.at[1, j, hb], zn(7))
    lwait(2)
    rotate(2)
    lfwd(2)
    recv("bpe", Bp.at[1, :, hb])
    recv("bme", Bm.at[1, :, ha])
    for s in (3, 4):
        for j in range(4):
            k = zi(5 - s)
            recv(("bp", s - 1, j), Bp.at[s - 2, j] if s > 3 else Bp.at[1, j, ha])
            Qs[k, j] = (Qf[k, j] + Bp[s - 2, j].astype(F32)).astype(BF16)
            send(("bp", s, j), Qs.at[k, j], Bp.at[s - 1, j], zn(1))
            k = zi(3 + s)
            recv(("bm", s - 1, j), Bm.at[s - 2, j] if s > 3 else Bm.at[1, j, hb])
            Qs[k, j] = (Qf[k, j] + Bm[s - 2, j].astype(F32)).astype(BF16)
            send(("bm", s, j), Qs.at[k, j], Bm.at[s - 1, j], zn(7))
        if s == 3:
            lshare(2)
            lwait(3)
            rotate(3)
    own[1].wait()
    own[2].wait()
    begin()
    for j in range(4):
        recv(("bp", 4, j), Bp.at[3, j])
        recv(("bm", 4, j), Bm.at[3, j])
        rows = slice(j * 128, (j + 1) * 128)
        rotated = (Qf[z, j] + Bp[3, j].astype(F32) + Bm[3, j].astype(F32)).T
        first = beta_one * mb[rows] + (1.0 - beta_one) * rotated
        second = beta_two * vb[rows] + (1.0 - beta_two) * rotated * rotated
        one = first * (1.0 / (1.0 - beta_one**STEP))
        two = second * (1.0 / (1.0 - beta_two**STEP))
        Sb[z, j] = (one / (jnp.sqrt(two) + epsilon)).astype(BF16)
        same(("cp", 1, j), Sb.at[z, j], zn(1))
        same(("cm", 1, j), Sb.at[z, j], zn(7))
        fb[rows] = first
        sb[rows] = second
    outs = [pltpu.make_async_copy(fb, fo, lsem.at[3]), pltpu.make_async_copy(sb, so, lsem.at[4])]
    for copy in outs:
        copy.start()

    def across(d):
        send(("ss", d), Sb.at[zi(d)], So.at[zi(d)], sib)

    def crossed(*ds):
        for d in ds:
            recv(("ss", d), So.at[zi(d)])

    def back(j):
        k = (zh + rels[j]) % 4
        s = jnp.concatenate(
            [ref[2 * k + i].reshape(512, 128) for ref in (Sb, So) for i in range(2)], axis=1)
        part = jnp.dot(left(j), s, preferred_element_type=F32)
        if j == 3:
            Ba[...] = part
        elif j > 0:
            Ba[...] += part
        else:
            Bk[...] = (Ba[...] + part).astype(BF16)

    across(0)
    for s in (2, 3):
        for j in range(4):
            recv(("cp", s - 1, j), Sb.at[zi(9 - s), j])
            same(("cp", s, j), Sb.at[zi(9 - s), j], zn(1))
            recv(("cm", s - 1, j), Sb.at[zi(s - 1), j])
            same(("cm", s, j), Sb.at[zi(s - 1), j], zn(7))
        across(9 - s)
        across(s - 1)
    crossed(0, 1, 7)
    back(3)
    for j in range(2):
        recv(("cp", 3, j), Sb.at[zi(5), j])
        same(("cp", 4, j), Sb.at[zi(5), j], zn(1))
        recv(("cm", 3, j + 2), Sb.at[zi(3), j + 2])
        same(("cm", 4, j + 2), Sb.at[zi(3), j + 2], zn(7))
    crossed(2, 6)
    back(2)
    for j in range(2):
        recv(("cp", 3, j + 2), Sb.at[zi(5), j + 2])
        recv(("cm", 3, j), Sb.at[zi(3), j])
    across(5)
    across(3)
    crossed(3, 5)
    back(1)
    for j in range(2):
        recv(("cp", 4, j), Sb.at[zi(4), j])
        recv(("cm", 4, j + 2), Sb.at[zi(4), j + 2])
    across(4)
    crossed(4)
    back(0)
    recv("rs0", Rs.at[zl])
    recv("rs1", Rs.at[1 - zl])
    def partial(k, pair_of_parts, is_own):
        rows = [pl.ds(pl.multiple_of((k // 2) * 512 + h * 256 + pair_of_parts * 128, 128), 128) for h in range(2)]
        n = pl.ds((k % 2) * 4, 4)
        lhs = jnp.concatenate([Bk[i, :] for i in rows], axis=0)
        rhs = jnp.concatenate(
            [Rb[i, n, c].reshape(512, 128) for i in range(2)] + [Rs[i, n].reshape(512, 128) for i in range(2)],
            axis=1)
        res = lax.dot_general(lhs, rhs, (((1,), (1,)), ((), ())), preferred_element_type=F32)
        for i in range(2):
            u = 2 * pair_of_parts + i
            top, low = res[i * 64:i * 64 + 64], res[128 + i * 64:192 + i * 64]
            kept = top[:, 0:128]
            for j in range(4):
                at = slice(j * 128, (j + 1) * 128)
                Vb[k, j, 0, u] = top[:, at].astype(BF16)
                if j > 0:
                    kept = jnp.where(y == j, top[:, at], kept)
                if is_own:
                    W[1, u, j] = low[:, at]
                else:
                    Vb[k, j, 1, u] = low[:, at].astype(BF16)
            W[0, u, k] = kept

    def send_far_x(u):
        send(("dx", 1, u), Vb.at[s2, lo, 1, u], Ra.at[1, u, 0], xn(1))
        send(("dx", 3, u), Vb.at[s2, hi, 1, u], Ra.at[1, u, 1], xn(3))

    def send_far_y(u):
        send(("dy", 1, u), Vb.at[lo, y2, 0, u], Ra.at[0, u, 0], yn(1))
        send(("dy", 3, u), Vb.at[hi, y2, 0, u], Ra.at[0, u, 1], yn(3))

    def send_near(u):
        for i, part, a, b, d in ((0, lo, sp, yp, 1), (1, hi, sm, ym, 3)):
            recv(("dx", d, u), Ra.at[1, u, i])
            Vb[a, part, 1, u] = (Vb[a, part, 1, u].astype(F32) + Ra[1, u, i].astype(F32)).astype(BF16)
            send(("nx", u), Vb.at[a, :, 1, u], Rd.at[1, u, i], xn(d))
            recv(("dy", d, u), Ra.at[0, u, i])
            Vb[part, b, 0, u] = (Vb[part, b, 0, u].astype(F32) + Ra[0, u, i].astype(F32)).astype(BF16)
            send(("ny", u), Vb.at[:, b, 0, u], Rd.at[0, u, i], yn(d))

    def send_small(u):
        for h, name, small, step in ((1, "nx", "ey", yn), (0, "ny", "ex", xn)):
            recv((name, u), Rd.at[h, u])
            total = W[h, u] + Rd[h, u, 0].astype(F32) + Rd[h, u, 1].astype(F32)
            W[h, u] = total
            Wb[h, u] = total.astype(BF16)
            for d in (2, 1, 3):
                at = (y + d) % 4 if h == 1 else (s0 + d) % 4
                send((small, u), Wb.at[h, u, at], X.at[h, u, d - 1], step(d))

    def send_final(u):
        for h, small, at in ((1, "ey", y), (0, "ex", s0)):
            recv((small, u), X.at[h, u])
            Fb[h, u] = W[h, u, at] + X[h, u, 0].astype(F32) + X[h, u, 1].astype(F32) + X[h, u, 2].astype(F32)
            send("f", Fb.at[h, u], upd.at[pl.ds(h * 256 + u * 64, 64)], final_to)

    begin()
    for i in range(2):
        partial(s2, i, False)
        send_far_x(2 * i)
        send_far_x(2 * i + 1)
        partial(sp, i, False)
        partial(sm, i, False)
        partial(s0, i, True)
        send_far_y(2 * i)
        send_far_y(2 * i + 1)
    send_near(0)
    send_near(1)
    send_small(0)
    send_near(2)
    send_small(1)
    send_near(3)
    send_final(0)
    send_small(2)
    send_final(1)
    send_small(3)
    send_final(2)
    send_final(3)
    @pl.when(g_slot != 0)
    def _():
        for h in range(2):
            move(h).wait_send()

    for phase in range(3):
        left_device(phase)
    recv("f", upd)
    for copy in outs:
        copy.wait()
    assert len(slots) <= SLOTS, len(slots)


def hand_over(a, b, c, a_out, b_out, c_out, buf, sem):
    there = [pltpu.make_async_copy(src, buf.at[i], sem.at[i]) for i, src in enumerate((a, b, c))]
    back = [pltpu.make_async_copy(buf.at[i], dst, sem.at[3 + i]) for i, dst in enumerate((a_out, b_out, c_out))]
    for copy in there:
        copy.start()
    for i in range(3):
        there[i].wait()
        back[i].start()
    for copy in back:
        copy.wait()


def body(gradient, first_moment, second_moment, left_basis, right_basis):
    hbm = pl.BlockSpec(memory_space=pl.ANY)
    vm = pltpu.VMEM
    update, first_new, second_new = pl.pallas_call(
        kernel,
        out_shape=(
            jax.ShapeDtypeStruct((512, 128), F32),
            jax.ShapeDtypeStruct((512, 128), F32),
            jax.ShapeDtypeStruct((512, 128), F32),
        ),
        in_specs=[hbm] * 5,
        out_specs=(hbm, hbm, hbm),
        scratch_shapes=[
            vm((2, 256, 128), BF16),
            vm((4, 4, 2, 2, 256, 128), BF16),
            vm((4, 4, 2, 4, 2, 32, 256), BF16),
            vm((2, 8, 2, 128, 128), BF16),
            vm((2, 8, 128, 128), BF16),
            vm((256, 1024), BF16),
            vm((8, 4, 128, 128), F32),
            vm((8, 4, 128, 128), BF16),
            vm((4, 4, 128, 128), BF16),
            vm((4, 4, 128, 128), BF16),
            vm((8, 4, 128, 128), BF16),
            vm((8, 4, 128, 128), BF16),
            vm((1024, 512), F32),
            vm((1024, 512), BF16),
            vm((4, 4, 2, 4, 64, 128), BF16),
            vm((2, 4, 2, 2, 64, 128), BF16),
            vm((2, 4, 2, 4, 64, 128), BF16),
            vm((2, 4, 4, 64, 128), F32),
            vm((2, 4, 4, 64, 128), BF16),
            vm((2, 4, 3, 64, 128), BF16),
            vm((2, 4, 64, 128), F32),
            vm((512, 128), F32),
            vm((512, 128), F32),
            vm((512, 128), F32),
            vm((512, 128), F32),
            pltpu.SemaphoreType.DMA((8,)),
            pltpu.SemaphoreType.DMA((SLOTS,)),
            pltpu.SemaphoreType.DMA((5,)),
            pltpu.SemaphoreType.DMA((4,)),
        ],
        compiler_params=pltpu.CompilerParams(
            collective_id=0, has_side_effects=True, vmem_limit_bytes=63 * 2**20),
        cost_estimate=pl.CostEstimate(flops=5 * 10**9, bytes_accessed=10**7, transcendentals=10**5),
    )(
        gradient.reshape(2, 256, 128),
        left_basis,
        right_basis.reshape(8, 2, 128, 128),
        first_moment,
        second_moment,
    )
    whole = jax.ShapeDtypeStruct((512, 128), F32)
    return pl.pallas_call(
        hand_over,
        out_shape=(whole, whole, whole),
        in_specs=[hbm] * 3,
        out_specs=(hbm, hbm, hbm),
        scratch_shapes=[vm((3, 512, 128), F32), pltpu.SemaphoreType.DMA((6,))],
        compiler_params=pltpu.CompilerParams(vmem_limit_bytes=63 * 2**20),
    )(update, first_new, second_new)


def solution(mesh):
    place = P("row", "col")
    placed = (place, place, place, P("col", "row"), place)
    return jax.shard_map(
        body, mesh=mesh, in_specs=placed, out_specs=(place, place, place), check_vma=False)
```
